128 devices in a mesh: dp: 32 (over z, x, core), pool: 4 (over y).
Axes of the slice: x: 4, y: 4, z: 4, core: 2. Of those that a mesh axis runs over, the one named last changes fastest.
Arguments:
- queries: float32 [1024, 4096], P(('dp', 'pool')), may hold values from -1 to 1, as said below
- documents: float32 [1024, 4096], P(('dp', 'pool')), may hold values from -1 to 1
- document_pool: float32 [65536, 4096], P(('dp', 'pool')), may hold values from -1 to 1
- hard_negatives: int32 [1024, 16], P(('dp', 'pool')), may hold values from 0 to 65535, as said below
Outputs:
- averaged_objective: float32 [], replicated
- query_grad: float32 [1024, 4096], P(('dp', 'pool'))
- document_grad: float32 [1024, 4096], P(('dp', 'pool'))
- pool_grad: float32 [65536, 4096], P(('dp', 'pool'))
The draws below stay inside these ranges and needn't reach their ends.
Inputs may be any that keep to these rules, and one draw needn't show every extreme that they name: `queries`: rows are noisy embeddings of several scales; entries lie in the stated range. `hard_negatives`: of the 128 ids held by one device, at most 2 lie in the rows k * 512 to (k + 1) * 512 - 1 for any k, and exactly 2 do so for at least 16 values of k; some ids repeat.
All inputs are finite; a program needn't handle non-finite values.
Results may differ from the reference program's by a relative error of at most 0.0003.
Values sent between devices are 32-bit elements; how exact they have to be, the bound alone decides.
No kernel may reach another device: no remote copies, remote signals or barrier semaphores. Data moves between devices by JAX's collectives and lax.ppermute only.
A program may use at most 128 MiB of HBM per device.

```python
import math
import jax
import jax.numpy as jnp
from jax import lax

D = 4096
HARD_NEGATIVES = 16
QUERY_DEV = 8
POOL_DEV = 512
BATCH = 1024
POOL = 65536
CAP = 2
DEVICES = 128


topic_count = 64


def topic_table(key):
    return jax.random.normal(jax.random.fold_in(key, 7), (topic_count, D), jnp.float32)


def query_topics(key):
    return jax.random.randint(jax.random.fold_in(key, 8), (BATCH,), 0, topic_count)


def mix_rows(centers, noise, scales):
    return jnp.clip(scales * (0.6 * centers + noise) / math.sqrt(D), -1.0, 1.0)


def draw_queries(key, part):
    centers = topic_table(key)[query_topics(key)]
    key = jax.random.fold_in(key, 11)
    first, second = jax.random.split(key, 2)
    noise = jax.random.normal(first, (BATCH, D), jnp.float32)
    scales = jnp.exp(jax.random.uniform(second, (BATCH, 1), jnp.float32, -1.2, 1.1))
    return mix_rows(centers, noise, scales)


def draw_documents(key, part):
    centers = topic_table(key)[query_topics(key)]
    key = jax.random.fold_in(key, 12)
    first, second = jax.random.split(key, 2)
    noise = jax.random.normal(first, (BATCH, D), jnp.float32)
    scales = jnp.exp(jax.random.uniform(second, (BATCH, 1), jnp.float32, -1.2, 1.1))
    return mix_rows(centers, noise, scales)


def draw_document_pool(key, part):
    centers = topic_table(key)[jnp.arange(POOL, dtype=jnp.int32) % topic_count]
    key = jax.random.fold_in(key, 13)
    first, second = jax.random.split(key, 2)
    noise = jax.random.normal(first, (POOL, D), jnp.float32)
    scales = jnp.exp(jax.random.uniform(second, (POOL, 1), jnp.float32, -1.2, 1.1))
    return mix_rows(centers, noise, scales)


def draw_hard_negatives(key, part):
    topics = query_topics(key)
    key = jax.random.fold_in(key, 14)
    key_hot, key_source, key_popular = jax.random.split(key, 3)
    hot_count = DEVICES // 8
    order = jax.random.permutation(key_hot, DEVICES)
    frequent_holders = order[:hot_count]
    cold_owners = order[hot_count:]
    cold_needed = QUERY_DEV * HARD_NEGATIVES - hot_count * CAP

    def one_source(source_key):
        first, second = jax.random.split(source_key)
        cold_slots = jax.random.permutation(first, jnp.tile(cold_owners, CAP))[:cold_needed]
        owner_list = jnp.concatenate([jnp.repeat(frequent_holders, CAP), cold_slots])
        return jax.random.permutation(second, owner_list)
    owners = jax.vmap(one_source)(jax.random.split(key_source, DEVICES)).reshape(BATCH, HARD_NEGATIVES)
    first, second = jax.random.split(key_popular)
    ceiling = jax.random.randint(first, (BATCH, HARD_NEGATIVES), 1, POOL_DEV // topic_count + 1)
    popular = jax.random.randint(second, (BATCH, HARD_NEGATIVES), 0, ceiling)
    return (owners * POOL_DEV + topics[:, None] + topic_count * popular).astype(jnp.int32)


def setup_inputs(seed: int = 0) -> dict:
    streams_of = jax.random.split(jax.random.key(seed), 5)
    return {
        "queries": draw_queries(jax.random.fold_in(streams_of[4], 71), 0),
        "documents": draw_documents(jax.random.fold_in(streams_of[4], 71), 0),
        "document_pool": draw_document_pool(jax.random.fold_in(streams_of[4], 71), 0),
        "hard_negatives": draw_hard_negatives(jax.random.fold_in(streams_of[4], 71), 0),
    }


inverse_heat_coefficient = 20.0
epsilon = 1e-06

def unit_rows(values):
    return values * lax.rsqrt(lax.optimization_barrier(jnp.sum(values * values, axis=-1, keepdims=True)) + epsilon)

def summed_loss(queries, documents, document_pool, hard_negatives):
    question_directions = unit_rows(queries)
    passage_direction = unit_rows(documents)
    distractor_directions = unit_rows(document_pool[hard_negatives])
    pairwise_affinity_grid = inverse_heat_coefficient * jnp.dot(question_directions, passage_direction.T, precision=lax.Precision.HIGHEST, preferred_element_type=jnp.float32)
    distractor_similarity = inverse_heat_coefficient * jnp.einsum('cz,coz->co', question_directions, distractor_directions, precision=lax.Precision.HIGHEST)
    normalizer_totals = lax.optimization_barrier(jnp.sum(jnp.exp(pairwise_affinity_grid - inverse_heat_coefficient), axis=1)) + lax.optimization_barrier(jnp.sum(jnp.exp(distractor_similarity - inverse_heat_coefficient), axis=1))
    per_instance_costs = jnp.log(normalizer_totals) + inverse_heat_coefficient - jnp.diagonal(pairwise_affinity_grid)
    return jnp.sum(per_instance_costs)

def reference(queries, documents, document_pool, hard_negatives):

    def wrapped(first, second, third):
        return summed_loss(first, second, third, hard_negatives)
    summed, pullback = jax.vjp(wrapped, queries, documents, document_pool)
    query_grad, document_grad, pool_grad = pullback(jnp.ones_like(summed))
    return (summed / BATCH, query_grad, document_grad, pool_grad)
```

```python
import jax
import jax.numpy as jnp
from jax import lax
from jax.sharding import PartitionSpec as P

heat = 20.0
epsilon = 1e-06
highest = lax.Precision.HIGHEST
everyone = ("dp", "pool")
capacity = 2


def factor_of(values):
    return lax.rsqrt(jnp.sum(values * values, axis=-1, keepdims=True) + epsilon)


def dot(left, right, contract, precision=highest):
    return lax.dot_general(
        left, right, (contract, ((), ())), precision=precision, preferred_element_type=jnp.float32
    )


def local(queries, documents, document_pool, hard_negatives):
    own, width = queries.shape
    pool_rows = document_pool.shape[0]
    neg = hard_negatives.shape[1]
    pool_size = lax.axis_size("pool")
    devices = lax.axis_size("dp") * pool_size
    batch = own * devices
    slots = devices * capacity
    ids = own * neg
    me = lax.axis_index("dp") * pool_size + lax.axis_index("pool")

    query_factor = factor_of(queries)
    doc_factor = factor_of(documents)
    query_unit = queries * query_factor
    doc_unit = documents * doc_factor

    flat = hard_negatives.reshape(-1)
    owner = flat // pool_rows
    order = jnp.arange(ids, dtype=jnp.int32)
    earlier = (owner[:, None] == owner[None, :]) & (order[None, :] < order[:, None])
    slot = owner * capacity + jnp.sum(earlier.astype(jnp.int32), axis=1)
    asker = order // neg
    code = (flat - owner * pool_rows) * own + asker
    taken = slot[None, :] == jnp.arange(slots, dtype=jnp.int32)[:, None]
    request = jnp.sum(jnp.where(taken, code[None, :] + 1, 0), axis=1) - 1
    slot_query = jnp.sum(jnp.where(taken, asker[None, :] + 1, 0), axis=1) - 1
    arrived = lax.all_to_all(
        request.reshape(devices, capacity), everyone, split_axis=0, concat_axis=0, tiled=True
    ).reshape(-1)
    valid = arrived >= 0
    wanted = jnp.maximum(arrived, 0)
    named_row = wanted // own
    named_query = jnp.arange(slots, dtype=jnp.int32) // capacity * own + wanted % own

    rows = jnp.take(document_pool, named_row, axis=0)
    row_factor = factor_of(rows)
    row_unit = rows * row_factor
    neg_rows = lax.all_to_all(row_unit, everyone, split_axis=0, concat_axis=0, tiled=True)

    cohort = lax.all_gather(query_unit, "pool", axis=0, tiled=True)
    passages = lax.all_gather(doc_unit, "dp", axis=0, tiled=True)
    everything = lax.all_gather(cohort, "dp", axis=0, tiled=True)
    parts = jnp.exp(heat * dot(cohort, passages, ((1,), (1,))) - heat)
    sums = jnp.sum(parts, axis=1, keepdims=True)
    mixed = dot(parts, passages, ((1,), (0,)))
    payload = jnp.concatenate([mixed, jnp.broadcast_to(sums, (sums.shape[0], 128))], axis=1)
    shares = lax.all_to_all(payload, "pool", split_axis=0, concat_axis=0, tiled=True)
    shares = jnp.sum(shares.reshape(pool_size, own, width + 128), axis=0)

    neg_scores = heat * dot(query_unit, neg_rows, ((1,), (1,)))
    asks = slot_query[None, :] == jnp.arange(own, dtype=jnp.int32)[:, None]
    neg_parts = jnp.where(asks, jnp.exp(neg_scores - heat), 0.0)
    totals = shares[:, width] + jnp.sum(neg_parts, axis=1)
    weighted = shares[:, :width] + dot(neg_parts, neg_rows, ((1,), (0,)))
    upstream = heat * (weighted / totals[:, None] - doc_unit)
    query_grad = query_factor * (
        upstream - query_unit * jnp.sum(query_unit * upstream, axis=-1, keepdims=True)
    )

    diagonal = heat * jnp.sum(query_unit * doc_unit, axis=1)
    slot_weight = heat * jnp.sum(neg_parts / totals[:, None], axis=0)
    news = jnp.concatenate(
        [
            jnp.broadcast_to(totals, (devices, own)),
            jnp.broadcast_to(diagonal, (devices, own)),
            slot_weight.reshape(devices, capacity),
        ],
        axis=1,
    )
    news = lax.all_to_all(news, everyone, split_axis=0, concat_axis=0, tiled=True)
    all_totals = news[:, :own].reshape(-1)
    all_diagonal = news[:, own : 2 * own].reshape(-1)
    weight = news[:, 2 * own :].reshape(-1)
    objective = jnp.sum(jnp.log(all_totals) + heat - all_diagonal) / batch

    number = jnp.arange(batch, dtype=jnp.int32)
    doc_parts = jnp.exp(heat * dot(doc_unit, everything, ((1,), (1,))) - heat)
    matched = (number[None, :] == me * own + jnp.arange(own, dtype=jnp.int32)[:, None]).astype(
        jnp.float32
    )
    doc_weight = heat * (doc_parts / all_totals[None, :] - matched)
    doc_upstream = dot(doc_weight, everything, ((1,), (0,)))
    document_grad = doc_factor * (
        doc_upstream - doc_unit * jnp.sum(doc_unit * doc_upstream, axis=-1, keepdims=True)
    )

    spread = jnp.where(named_query[:, None] == number[None, :], weight[:, None], 0.0)
    same = (named_row[:, None] == named_row[None, :]) & valid[None, :]
    spread = dot(same.astype(jnp.float32), spread, ((1,), (0,)))
    row_upstream = dot(spread, everything, ((1,), (0,)))
    row_grad = row_factor * (
        row_upstream - row_unit * jnp.sum(row_unit * row_upstream, axis=-1, keepdims=True)
    )
    pool_grad = (
        jnp.zeros((pool_rows, width), jnp.float32)
        .at[jnp.where(valid, named_row, pool_rows)]
        .set(row_grad, mode="drop")
    )
    return (objective, query_grad, document_grad, pool_grad)


def solution(mesh):
    rows = P(everyone, None)
    return jax.shard_map(
        local,
        mesh=mesh,
        in_specs=(rows, rows, rows, rows),
        out_specs=(P(), rows, rows, rows),
        check_vma=False,
    )
```

```python
import functools

import jax
import jax.numpy as jnp
from jax import lax
from jax.experimental import pallas as pl
from jax.experimental.pallas import tpu as pltpu
from jax.sharding import PartitionSpec as P

heat = 20.0
epsilon = 1e-06
highest = lax.Precision.HIGHEST
lanes = 128
everyone = ("dp", "pool")
capacity = 2
limit = 56 * 1024 * 1024


def halves(values):
    high = values.astype(jnp.bfloat16)
    return high, (values - high.astype(jnp.float32)).astype(jnp.bfloat16)


def dot3(left, right, contract):
    one = lambda a, b: lax.dot_general(
        a, b, (contract, ((), ())), preferred_element_type=jnp.float32
    )
    return one(left[0], right[0]) + (one(left[0], right[1]) + one(left[1], right[0]))


def pick_kernel(step_rows, wanted, pool, unit, factor, packed, held, arrived):
    step = pl.program_id(0)
    width = pool.shape[1]
    strips = width // lanes
    total = held.shape[0]

    @pl.when(step == 0)
    def _():
        def fetch(j, carry):
            pltpu.make_async_copy(
                pool.at[pl.ds(wanted[j], 1)], held.at[pl.ds(j, 1)], arrived.at[j // step_rows]
            ).start()
            return carry

        lax.fori_loop(0, total, fetch, 0, unroll=8)

    start = pl.multiple_of(step * step_rows, step_rows)
    pltpu.make_async_copy(
        pool.at[pl.ds(0, step_rows)], held.at[pl.ds(start, step_rows)], arrived.at[step]
    ).wait()
    for tile in range(step_rows // 8):
        rows = held[pl.ds(start + tile * 8, 8), :]
        scale = lax.rsqrt(jnp.sum(rows * rows, axis=1, keepdims=True) + epsilon)
        rows = rows * scale
        unit[pl.ds(tile * 8, 8), :] = rows
        factor[pl.ds(tile * 8, 8), :] = jnp.broadcast_to(scale, (8, lanes))
        for strip in range(strips):
            packed[pl.ds(tile * 8 * strips + strip, 8, stride=strips), :] = rows[
                :, strip * lanes : (strip + 1) * lanes
            ]


def pick(wanted, pool):
    total = wanted.shape[0]
    width = pool.shape[1]
    strips = width // lanes
    step_rows = 32
    return pl.pallas_call(
        functools.partial(pick_kernel, step_rows),
        grid_spec=pltpu.PrefetchScalarGridSpec(
            num_scalar_prefetch=1,
            grid=(total // step_rows,),
            in_specs=[pl.BlockSpec(memory_space=pl.ANY)],
            out_specs=[
                pl.BlockSpec((step_rows, width), lambda i, *_: (i, 0)),
                pl.BlockSpec((step_rows, lanes), lambda i, *_: (i, 0)),
                pl.BlockSpec((step_rows * strips, lanes), lambda i, *_: (i, 0)),
            ],
            scratch_shapes=[
                pltpu.VMEM((total, width), jnp.float32),
                pltpu.SemaphoreType.DMA((total // step_rows,)),
            ],
        ),
        out_shape=[
            jax.ShapeDtypeStruct((total, width), jnp.float32),
            jax.ShapeDtypeStruct((total, lanes), jnp.float32),
            jax.ShapeDtypeStruct((total * strips, lanes), jnp.float32),
        ],
        compiler_params=pltpu.CompilerParams(vmem_limit_bytes=limit),
        cost_estimate=pl.CostEstimate(flops=4 * total * width, bytes_accessed=12 * total * width, transcendentals=0),
    )(wanted, pool)


def against_kernel(packed, unit, asker, parts, mixed, rows):
    strips = rows.shape[1] // lanes
    count = rows.shape[0]
    for strip in range(strips):
        rows[:, strip * lanes : (strip + 1) * lanes] = packed[pl.ds(strip, count, stride=strips), :]
    split = halves(rows[...])
    scores = heat * dot3(halves(unit[...]), split, ((1,), (1,)))
    number = lax.broadcasted_iota(jnp.int32, scores.shape, 0)
    chosen = jnp.where(asker[...] == number, jnp.exp(scores - heat), 0.0)
    parts[...] = chosen
    mixed[...] = dot3(halves(chosen), split, ((1,), (0,)))


def against(packed, unit, asker):
    own, width = unit.shape
    count = packed.shape[0] // (width // lanes)
    return pl.pallas_call(
        against_kernel,
        out_shape=[
            jax.ShapeDtypeStruct((own, count), jnp.float32),
            jax.ShapeDtypeStruct((own, width), jnp.float32),
        ],
        scratch_shapes=[pltpu.VMEM((count, width), jnp.float32)],
        compiler_params=pltpu.CompilerParams(vmem_limit_bytes=limit),
        cost_estimate=pl.CostEstimate(flops=12 * own * count * width, bytes_accessed=4 * count * width, transcendentals=0),
    )(packed, unit, asker)


def finish_kernel(
    target, weight, queries, unit, factor, doc_unit, doc_factor,
    doc_grad, pool_grad, upstream, high, low, blank, fill_sem, row_sem,
):
    step = pl.program_id(0)
    block = queries.shape[1]
    slots = unit.shape[0]
    own = doc_unit.shape[0]
    blank_rows = blank.shape[0]
    fills = [
        pltpu.make_async_copy(blank, pool_grad.at[pl.ds(i * blank_rows, blank_rows)], fill_sem.at[i])
        for i in range(pool_grad.shape[0] // blank_rows)
    ]

    @pl.when(step == 0)
    def _():
        blank[...] = jnp.zeros_like(blank)
        for fill in fills:
            fill.start()
        first, second = halves(weight[...])
        high[...] = first
        low[...] = second

    right = halves(queries[...])
    column = pl.multiple_of(step * block, block)
    upstream[:, pl.ds(column, block)] = dot3((high[...], low[...]), right, ((1,), (0,)))

    @pl.when(step == pl.num_programs(0) - 1)
    def _():
        for fill in fills:
            fill.wait()
        above = upstream[pl.ds(slots, own), :]
        inner = jnp.sum(doc_unit[...] * above, axis=1, keepdims=True)
        doc_grad[...] = doc_factor[:, :1] * (above - doc_unit[...] * inner)

        def row_copy(j):
            return pltpu.make_async_copy(
                upstream.at[pl.ds(j, 1)], pool_grad.at[pl.ds(target[j], 1)], row_sem
            )

        def settle(tile, carry):
            rows = pl.ds(pl.multiple_of(tile * 8, 8), 8)
            above = upstream[rows, :]
            unit_rows = unit[rows, :]
            inner = jnp.sum(unit_rows * above, axis=1, keepdims=True)
            upstream[rows, :] = factor[rows, :1] * (above - unit_rows * inner)
            for i in range(8):
                @pl.when(target[tile * 8 + i] >= 0)
                def _():
                    row_copy(tile * 8 + i).start()
            return carry

        lax.fori_loop(0, slots // 8, settle, 0)

        def drain(j, carry):
            @pl.when(target[j] >= 0)
            def _():
                row_copy(j).wait()
            return carry

        lax.fori_loop(0, slots, drain, 0)


def finish(target, weight, queries, unit, factor, doc_unit, doc_factor, pool_rows):
    slots, width = unit.shape
    own = doc_unit.shape[0]
    batch = queries.shape[0]
    block = 512
    whole = lambda a: pl.BlockSpec(a.shape, lambda i, *_: (0, 0))
    blank_rows = 64
    return pl.pallas_call(
        finish_kernel,
        grid_spec=pltpu.PrefetchScalarGridSpec(
            num_scalar_prefetch=1,
            grid=(width // block,),
            in_specs=[
                whole(weight),
                pl.BlockSpec((batch, block), lambda i, *_: (0, i)),
                whole(unit),
                whole(factor),
                whole(doc_unit),
                whole(doc_factor),
            ],
            out_specs=[whole(doc_unit), pl.BlockSpec(memory_space=pl.ANY)],
            scratch_shapes=[
                pltpu.VMEM((slots + own, width), jnp.float32),
                pltpu.VMEM((slots + own, batch), jnp.bfloat16),
                pltpu.VMEM((slots + own, batch), jnp.bfloat16),
                pltpu.VMEM((blank_rows, width), jnp.float32),
                pltpu.SemaphoreType.DMA((pool_rows // blank_rows,)),
                pltpu.SemaphoreType.DMA,
            ],
        ),
        out_shape=[
            jax.ShapeDtypeStruct((own, width), jnp.float32),
            jax.ShapeDtypeStruct((pool_rows, width), jnp.float32),
        ],
        compiler_params=pltpu.CompilerParams(vmem_limit_bytes=limit),
        cost_estimate=pl.CostEstimate(
            flops=6 * (slots + own) * batch * width, bytes_accessed=4 * width * (batch + pool_rows + slots), transcendentals=0
        ),
    )(target, weight, queries, unit, factor, doc_unit, doc_factor)


def factor_of(values):
    return lax.rsqrt(jnp.sum(values * values, axis=-1, keepdims=True) + epsilon)


def dot(left, right, contract):
    return lax.dot_general(
        left, right, (contract, ((), ())), precision=highest, preferred_element_type=jnp.float32
    )


def back(factor, unit, upstream):
    return factor * (upstream - unit * jnp.sum(unit * upstream, axis=-1, keepdims=True))


def local(queries, documents, document_pool, hard_negatives):
    own, width = queries.shape
    strips = width // lanes
    pool_rows = document_pool.shape[0]
    neg = hard_negatives.shape[1]
    pool_size = lax.axis_size("pool")
    groups = lax.axis_size("dp")
    devices = groups * pool_size
    batch = own * devices
    slots = devices * capacity
    ids = own * neg
    member = lax.axis_index("pool")
    me = lax.axis_index("dp") * pool_size + member

    def forward(values, steps):
        return lax.ppermute(
            values, "pool", [(i, (i + steps) % pool_size) for i in range(pool_size)]
        )

    def exchange(values):
        return lax.all_to_all(values, everyone, split_axis=0, concat_axis=0, tiled=True)

    flat = hard_negatives.reshape(-1)
    owner = flat // pool_rows
    order = jnp.arange(ids, dtype=jnp.int32)
    earlier = (owner[:, None] == owner[None, :]) & (order[None, :] < order[:, None])
    slot = owner * capacity + jnp.sum(earlier.astype(jnp.int32), axis=1)
    asker = order // neg
    code = (flat - owner * pool_rows) * own + asker
    taken = slot[None, :] == jnp.arange(slots, dtype=jnp.int32)[:, None]
    request = jnp.sum(jnp.where(taken, code[None, :] + 1, 0), axis=1) - 1
    slot_query = jnp.sum(jnp.where(taken, asker[None, :] + 1, 0), axis=1) - 1
    arrived = exchange(request.reshape(devices, capacity)).reshape(-1)

    query_factor = factor_of(queries)
    doc_factor = factor_of(documents)
    doc_unit = documents * doc_factor
    query_unit, arrived = lax.optimization_barrier((queries * query_factor, arrived))

    valid = arrived >= 0
    wanted = jnp.maximum(arrived, 0)
    named_row = wanted // own
    source = jnp.arange(slots, dtype=jnp.int32) // capacity
    place = (
        source // pool_size * pool_size + (source - member) % pool_size
    ) * own + wanted % own
    row_unit, row_factor, packed = pick(named_row, document_pool)
    neg_rows = exchange(packed.reshape(devices, capacity * strips, lanes))

    cohort = jnp.concatenate(
        [query_unit] + [forward(query_unit, -steps) for steps in range(1, pool_size)], axis=0
    )
    passages = lax.all_gather(doc_unit, "dp", axis=0, tiled=True)
    everything = lax.all_gather(cohort, "dp", axis=0, tiled=True)

    parts = jnp.exp(heat * dot(cohort, passages, ((1,), (1,))) - heat)
    sums = jnp.sum(parts, axis=1, keepdims=True)
    mixed = dot(parts, passages, ((1,), (0,)))
    payload = jnp.concatenate([mixed, jnp.broadcast_to(sums, (sums.shape[0], lanes))], axis=1)
    shares = payload[:own]
    for steps in range(1, pool_size):
        shares = shares + forward(payload[steps * own : (steps + 1) * own], steps)

    neg_parts, neg_mixed = against(
        neg_rows.reshape(slots * strips, lanes), query_unit, slot_query[None, :]
    )
    totals = shares[:, width] + jnp.sum(neg_parts, axis=1)
    upstream = heat * ((shares[:, :width] + neg_mixed) / totals[:, None] - doc_unit)
    query_grad = back(query_factor, query_unit, upstream)

    diagonal = heat * jnp.sum(query_unit * doc_unit, axis=1)
    slot_weight = heat * jnp.sum(neg_parts / totals[:, None], axis=0)
    block = parts.reshape(own * pool_size, groups, own).transpose(1, 2, 0).reshape(groups, 1, -1)
    here = jnp.arange(pool_size, dtype=jnp.int32)[None, :, None] == member
    news = jnp.concatenate(
        [
            jnp.where(here, block, 0.0).reshape(devices, -1),
            jnp.broadcast_to(totals, (devices, own)),
            jnp.broadcast_to(diagonal, (devices, own)),
            slot_weight.reshape(devices, capacity),
        ],
        axis=1,
    )
    news = exchange(news)
    edge = own * own * pool_size
    doc_parts = jnp.sum(news[:, :edge].reshape(groups, pool_size, edge), axis=1)
    doc_parts = doc_parts.reshape(groups, own, own * pool_size).transpose(1, 0, 2)
    all_totals = news[:, edge : edge + own]
    all_diagonal = news[:, edge + own : edge + 2 * own]
    slot_weight = news[:, edge + 2 * own :].reshape(-1)
    objective = jnp.sum(jnp.log(all_totals) + heat - all_diagonal) / batch
    placed_totals = jnp.roll(
        all_totals.reshape(groups, pool_size, own), -member, axis=1
    ).reshape(batch)

    number = jnp.arange(batch, dtype=jnp.int32)
    row = jnp.arange(own, dtype=jnp.int32)[:, None]
    matched = number[None, :] == me // pool_size * pool_size * own + row
    doc_weight = heat * (
        doc_parts.reshape(own, batch) / placed_totals[None, :] - matched.astype(jnp.float32)
    )
    spread = jnp.where(place[:, None] == number[None, :], slot_weight[:, None], 0.0)
    same = (named_row[:, None] == named_row[None, :]) & valid[None, :]
    spread = dot(same.astype(jnp.float32), spread, ((1,), (0,)))
    slot_order = jnp.arange(slots, dtype=jnp.int32)
    repeated = jnp.any(same & (slot_order[None, :] < slot_order[:, None]), axis=1)
    target = jnp.where(valid & ~repeated, named_row, -1)
    document_grad, pool_grad = finish(
        target,
        jnp.concatenate([spread, doc_weight], axis=0),
        everything,
        row_unit,
        row_factor,
        doc_unit,
        jnp.broadcast_to(doc_factor, (own, lanes)),
        pool_rows,
    )
    return (objective, query_grad, document_grad, pool_grad)


def solution(mesh):
    rows = P(everyone, None)
    return jax.shard_map(
        local,
        mesh=mesh,
        in_specs=(rows, rows, rows, rows),
        out_specs=(P(), rows, rows, rows),
        check_vma=False,
    )
```

```python
import functools

import jax
import jax.numpy as jnp
from jax import lax
from jax.experimental import pallas as pl
from jax.experimental.pallas import tpu as pltpu
from jax.sharding import PartitionSpec as P

heat = 20.0
epsilon = 1e-06
highest = lax.Precision.HIGHEST
lanes = 128
everyone = ("dp", "pool")
capacity = 2
limit = 56 * 1024 * 1024


def halves(values):
    high = values.astype(jnp.bfloat16)
    return high, (values - high.astype(jnp.float32)).astype(jnp.bfloat16)


def dot3(left, right, contract):
    one = lambda a, b: lax.dot_general(
        a, b, (contract, ((), ())), preferred_element_type=jnp.float32
    )
    return one(left[0], right[0]) + (one(left[0], right[1]) + one(left[1], right[0]))


def pick_kernel(step_rows, wanted, pool, unit, factor, packed, held, arrived):
    step = pl.program_id(0)
    width = pool.shape[1]
    strips = width // lanes
    total = held.shape[0]

    @pl.when(step == 0)
    def _():
        def fetch(j, carry):
            pltpu.make_async_copy(
                pool.at[pl.ds(wanted[j], 1)], held.at[pl.ds(j, 1)], arrived.at[j // step_rows]
            ).start()
            return carry

        lax.fori_loop(0, total, fetch, 0, unroll=8)

    start = pl.multiple_of(step * step_rows, step_rows)
    pltpu.make_async_copy(
        pool.at[pl.ds(0, step_rows)], held.at[pl.ds(start, step_rows)], arrived.at[step]
    ).wait()
    for tile in range(step_rows // 8):
        rows = held[pl.ds(start + tile * 8, 8), :]
        scale = lax.rsqrt(jnp.sum(rows * rows, axis=1, keepdims=True) + epsilon)
        rows = rows * scale
        unit[pl.ds(tile * 8, 8), :] = rows
        factor[pl.ds(tile * 8, 8), :] = jnp.broadcast_to(scale, (8, lanes))
        for strip in range(strips):
            packed[pl.ds(tile * 8 * strips + strip, 8, stride=strips), :] = rows[
                :, strip * lanes : (strip + 1) * lanes
            ]


def pick(wanted, pool):
    total = wanted.shape[0]
    width = pool.shape[1]
    strips = width // lanes
    step_rows = 32
    return pl.pallas_call(
        functools.partial(pick_kernel, step_rows),
        grid_spec=pltpu.PrefetchScalarGridSpec(
            num_scalar_prefetch=1,
            grid=(total // step_rows,),
            in_specs=[pl.BlockSpec(memory_space=pl.ANY)],
            out_specs=[
                pl.BlockSpec((step_rows, width), lambda i, *_: (i, 0)),
                pl.BlockSpec((step_rows, lanes), lambda i, *_: (i, 0)),
                pl.BlockSpec((step_rows * strips, lanes), lambda i, *_: (i, 0)),
            ],
            scratch_shapes=[
                pltpu.VMEM((total, width), jnp.float32),
                pltpu.SemaphoreType.DMA((total // step_rows,)),
            ],
        ),
        out_shape=[
            jax.ShapeDtypeStruct((total, width), jnp.float32),
            jax.ShapeDtypeStruct((total, lanes), jnp.float32),
            jax.ShapeDtypeStruct((total * strips, lanes), jnp.float32),
        ],
        compiler_params=pltpu.CompilerParams(vmem_limit_bytes=limit),
        cost_estimate=pl.CostEstimate(flops=4 * total * width, bytes_accessed=12 * total * width, transcendentals=0),
    )(wanted, pool)


def against_kernel(packed, unit, asker, parts, mixed, blank, rows, zeros, fill_sem):
    strips = rows.shape[1] // lanes
    count = rows.shape[0]
    zero_rows = zeros.shape[0]
    zeros[...] = jnp.zeros_like(zeros)
    fills = [
        pltpu.make_async_copy(zeros, blank.at[pl.ds(i * zero_rows, zero_rows)], fill_sem.at[i])
        for i in range(blank.shape[0] // zero_rows)
    ]
    for fill in fills:
        fill.start()
    for strip in range(strips):
        rows[:, strip * lanes : (strip + 1) * lanes] = packed[pl.ds(strip, count, stride=strips), :]
    split = halves(rows[...])
    scores = heat * dot3(halves(unit[...]), split, ((1,), (1,)))
    number = lax.broadcasted_iota(jnp.int32, scores.shape, 0)
    chosen = jnp.where(asker[...] == number, jnp.exp(scores - heat), 0.0)
    parts[...] = chosen
    mixed[...] = dot3(halves(chosen), split, ((1,), (0,)))
    for fill in fills:
        fill.wait()


def against(packed, unit, asker, pool_rows):
    own, width = unit.shape
    count = packed.shape[0] // (width // lanes)
    zero_rows = 64
    vmem = pl.BlockSpec(memory_space=pltpu.VMEM)
    return pl.pallas_call(
        against_kernel,
        out_specs=[vmem, vmem, pl.BlockSpec(memory_space=pl.ANY)],
        out_shape=[
            jax.ShapeDtypeStruct((own, count), jnp.float32),
            jax.ShapeDtypeStruct((own, width), jnp.float32),
            jax.ShapeDtypeStruct((pool_rows, width), jnp.float32),
        ],
        scratch_shapes=[
            pltpu.VMEM((count, width), jnp.float32),
            pltpu.VMEM((zero_rows, width), jnp.float32),
            pltpu.SemaphoreType.DMA((pool_rows // zero_rows,)),
        ],
        compiler_params=pltpu.CompilerParams(vmem_limit_bytes=limit),
        cost_estimate=pl.CostEstimate(
            flops=12 * own * count * width, bytes_accessed=4 * width * (count + pool_rows), transcendentals=0
        ),
    )(packed, unit, asker)


def finish_kernel(
    block, count, slot_of, row_of, weight, queries, unit, factor, doc_unit, doc_factor, blank,
    doc_grad, pool_grad, held, units, upstream, inner, high, low, query_sem, unit_sem, row_sem,
):
    slots, width = unit.shape
    own = doc_unit.shape[0]

    def columns(i):
        return pl.ds(pl.multiple_of(i * block, block), block)

    def query_copy(i):
        return pltpu.make_async_copy(
            queries.at[:, columns(i)], held.at[:, columns(i)], query_sem.at[i]
        )

    def unit_copy(i):
        return pltpu.make_async_copy(unit.at[:, columns(i)], units.at[:, columns(i)], unit_sem.at[i])

    for i in range(width // block):
        query_copy(i).start()
        unit_copy(i).start()
    inner[...] = jnp.zeros_like(inner)
    first, second = halves(weight[...])
    high[...] = first
    low[...] = second

    def multiply(i, carry):
        query_copy(i).wait()
        unit_copy(i).wait()
        above = dot3((high[...], low[...]), halves(held[:, columns(i)]), ((1,), (0,)))
        upstream[:, columns(i)] = above
        product = above[:slots] * units[:, columns(i)]
        part = product[:, :lanes]
        for strip in range(1, block // lanes):
            part = part + product[:, strip * lanes : (strip + 1) * lanes]
        inner[...] += part
        return carry

    lax.fori_loop(0, width // block, multiply, 0)

    above = upstream[pl.ds(slots, own), :]
    along = jnp.sum(doc_unit[...] * above, axis=1, keepdims=True)
    doc_grad[...] = doc_factor[:, :1] * (above - doc_unit[...] * along)

    def settle(tile, carry):
        rows = pl.ds(pl.multiple_of(tile * 16, 16), 16)
        along = jnp.sum(inner[rows, :], axis=1, keepdims=True)
        upstream[rows, :] = factor[rows, :1] * (upstream[rows, :] - units[rows, :] * along)
        return carry

    lax.fori_loop(0, slots // 16, settle, 0)

    def row_copy(j):
        return pltpu.make_async_copy(
            upstream.at[pl.ds(slot_of[j], 1)], pool_grad.at[pl.ds(row_of[j], 1)], row_sem
        )

    def send(j, carry):
        row_copy(j).start()
        return carry

    def drain(j, carry):
        row_copy(j).wait()
        return carry

    lax.fori_loop(0, count[0], send, 0)
    lax.fori_loop(0, count[0], drain, 0)


def finish(count, slot_of, row_of, weight, queries, unit, factor, doc_unit, doc_factor, blank):
    slots, width = unit.shape
    own = doc_unit.shape[0]
    batch = queries.shape[0]
    block = 512
    total = slots + 2 * own
    weight = jnp.pad(weight, ((0, total - weight.shape[0]), (0, 0)))
    vmem = pl.BlockSpec(memory_space=pltpu.VMEM)
    anywhere = pl.BlockSpec(memory_space=pl.ANY)
    smem = pl.BlockSpec(memory_space=pltpu.SMEM)
    return pl.pallas_call(
        functools.partial(finish_kernel, block),
        in_specs=[smem, smem, smem, vmem, anywhere, anywhere, vmem, vmem, vmem, anywhere],
        out_specs=[vmem, anywhere],
        scratch_shapes=[
            pltpu.VMEM((batch, width), jnp.float32),
            pltpu.VMEM((slots, width), jnp.float32),
            pltpu.VMEM((total, width), jnp.float32),
            pltpu.VMEM((slots, lanes), jnp.float32),
            pltpu.VMEM((total, batch), jnp.bfloat16),
            pltpu.VMEM((total, batch), jnp.bfloat16),
            pltpu.SemaphoreType.DMA((width // block,)),
            pltpu.SemaphoreType.DMA((width // block,)),
            pltpu.SemaphoreType.DMA,
        ],
        out_shape=[
            jax.ShapeDtypeStruct((own, width), jnp.float32),
            jax.ShapeDtypeStruct(blank.shape, jnp.float32),
        ],
        input_output_aliases={9: 1},
        compiler_params=pltpu.CompilerParams(vmem_limit_bytes=limit),
        cost_estimate=pl.CostEstimate(
            flops=6 * total * batch * width, bytes_accessed=4 * width * (batch + 2 * slots), transcendentals=0
        ),
    )(count, slot_of, row_of, weight, queries, unit, factor, doc_unit, doc_factor, blank)


def factor_of(values):
    return lax.rsqrt(jnp.sum(values * values, axis=-1, keepdims=True) + epsilon)


def dot(left, right, contract):
    return lax.dot_general(
        left, right, (contract, ((), ())), precision=highest, preferred_element_type=jnp.float32
    )


def back(factor, unit, upstream):
    return factor * (upstream - unit * jnp.sum(unit * upstream, axis=-1, keepdims=True))


def local(queries, documents, document_pool, hard_negatives):
    own, width = queries.shape
    strips = width // lanes
    pool_rows = document_pool.shape[0]
    neg = hard_negatives.shape[1]
    pool_size = lax.axis_size("pool")
    groups = lax.axis_size("dp")
    devices = groups * pool_size
    batch = own * devices
    slots = devices * capacity
    ids = own * neg
    member = lax.axis_index("pool")
    me = lax.axis_index("dp") * pool_size + member

    def forward(values, steps):
        return lax.ppermute(
            values, "pool", [(i, (i + steps) % pool_size) for i in range(pool_size)]
        )

    def exchange(values):
        return lax.all_to_all(values, everyone, split_axis=0, concat_axis=0, tiled=True)

    flat = hard_negatives.reshape(-1)
    owner = flat // pool_rows
    order = jnp.arange(ids, dtype=jnp.int32)
    earlier = (owner[:, None] == owner[None, :]) & (order[None, :] < order[:, None])
    slot = owner * capacity + jnp.sum(earlier.astype(jnp.int32), axis=1)
    asker = order // neg
    code = (flat - owner * pool_rows) * own + asker
    taken = slot[None, :] == jnp.arange(slots, dtype=jnp.int32)[:, None]
    request = jnp.sum(jnp.where(taken, code[None, :] + 1, 0), axis=1) - 1
    slot_query = jnp.sum(jnp.where(taken, asker[None, :] + 1, 0), axis=1) - 1
    request = request.reshape(devices, capacity)
    request = jnp.pad(request, ((0, 0), (0, lanes - capacity)), constant_values=-1)
    arrived = exchange(request)[:, :capacity].reshape(-1)

    query_factor = factor_of(queries)
    doc_factor = factor_of(documents)
    doc_unit = documents * doc_factor
    query_unit, arrived = lax.optimization_barrier((queries * query_factor, arrived))

    valid = arrived >= 0
    wanted = jnp.maximum(arrived, 0)
    named_row = wanted // own
    source = jnp.arange(slots, dtype=jnp.int32) // capacity
    place = (
        source // pool_size * pool_size + (source - member) % pool_size
    ) * own + wanted % own
    row_unit, row_factor, packed = pick(named_row, document_pool)
    neg_rows = exchange(packed.reshape(devices, capacity * strips, lanes))

    cohort = jnp.concatenate(
        [query_unit] + [forward(query_unit, -steps) for steps in range(1, pool_size)], axis=0
    )
    passages = lax.all_gather(doc_unit, "dp", axis=0, tiled=True)
    everything = lax.all_gather(cohort, "dp", axis=0, tiled=True)

    parts = jnp.exp(heat * dot(cohort, passages, ((1,), (1,))) - heat)
    sums = jnp.sum(parts, axis=1, keepdims=True)
    mixed = dot(parts, passages, ((1,), (0,)))
    payload = jnp.concatenate([mixed, jnp.broadcast_to(sums, (sums.shape[0], lanes))], axis=1)
    shares = payload[:own]
    for steps in range(1, pool_size):
        shares = shares + forward(payload[steps * own : (steps + 1) * own], steps)

    shares, slot_query = lax.optimization_barrier((shares, slot_query))
    neg_parts, neg_mixed, blank = against(
        neg_rows.reshape(slots * strips, lanes), query_unit, slot_query[None, :], pool_rows
    )
    totals = shares[:, width] + jnp.sum(neg_parts, axis=1)
    upstream = heat * ((shares[:, :width] + neg_mixed) / totals[:, None] - doc_unit)
    query_grad = back(query_factor, query_unit, upstream)

    diagonal = heat * jnp.sum(query_unit * doc_unit, axis=1)
    slot_weight = heat * jnp.sum(neg_parts / totals[:, None], axis=0)
    block = parts.reshape(own * pool_size, groups, own).transpose(1, 2, 0).reshape(groups, 1, -1)
    here = jnp.arange(pool_size, dtype=jnp.int32)[None, :, None] == member
    news = jnp.concatenate(
        [
            jnp.where(here, block, 0.0).reshape(devices, -1),
            jnp.broadcast_to(totals, (devices, own)),
            jnp.broadcast_to(diagonal, (devices, own)),
            slot_weight.reshape(devices, capacity),
        ],
        axis=1,
    )
    news = exchange(news)
    edge = own * own * pool_size
    doc_parts = jnp.sum(news[:, :edge].reshape(groups, pool_size, edge), axis=1)
    doc_parts = doc_parts.reshape(groups, own, own * pool_size).transpose(1, 0, 2)
    all_totals = news[:, edge : edge + own]
    all_diagonal = news[:, edge + own : edge + 2 * own]
    slot_weight = news[:, edge + 2 * own :].reshape(-1)
    objective = jnp.sum(jnp.log(all_totals) + heat - all_diagonal) / batch
    placed_totals = jnp.roll(
        all_totals.reshape(groups, pool_size, own), -member, axis=1
    ).reshape(batch)

    number = jnp.arange(batch, dtype=jnp.int32)
    row = jnp.arange(own, dtype=jnp.int32)[:, None]
    matched = number[None, :] == me // pool_size * pool_size * own + row
    doc_weight = heat * (
        doc_parts.reshape(own, batch) / placed_totals[None, :] - matched.astype(jnp.float32)
    )
    spread = jnp.where(place[:, None] == number[None, :], slot_weight[:, None], 0.0)
    same = (named_row[:, None] == named_row[None, :]) & valid[None, :]
    spread = dot(same.astype(jnp.float32), spread, ((1,), (0,)))
    slot_order = jnp.arange(slots, dtype=jnp.int32)
    repeated = jnp.any(same & (slot_order[None, :] < slot_order[:, None]), axis=1)
    written = valid & ~repeated
    rank = jnp.cumsum(written.astype(jnp.int32)) - 1
    listed = (rank[None, :] == slot_order[:, None]) & written[None, :]
    slot_of = jnp.sum(jnp.where(listed, slot_order[None, :], 0), axis=1)
    row_of = jnp.sum(jnp.where(listed, named_row[None, :], 0), axis=1)
    document_grad, pool_grad = finish(
        jnp.sum(written.astype(jnp.int32))[None],
        slot_of,
        row_of,
        jnp.concatenate([spread, doc_weight], axis=0),
        everything,
        row_unit,
        row_factor,
        doc_unit,
        jnp.broadcast_to(doc_factor, (own, lanes)),
        blank,
    )
    return (objective, query_grad, document_grad, pool_grad)


def solution(mesh):
    rows = P(everyone, None)
    return jax.shard_map(
        local,
        mesh=mesh,
        in_specs=(rows, rows, rows, rows),
        out_specs=(P(), rows, rows, rows),
        check_vma=False,
    )
```

```python
import functools

import jax
import jax.numpy as jnp
from jax import lax
from jax.experimental import pallas as pl
from jax.experimental.pallas import tpu as pltpu
from jax.sharding import PartitionSpec as P

heat = 20.0
epsilon = 1e-06
highest = lax.Precision.HIGHEST
lanes = 128
everyone = ("dp", "pool")
capacity = 2
limit = 56 * 1024 * 1024


def halves(values):
    high = values.astype(jnp.bfloat16)
    return high, (values - high.astype(jnp.float32)).astype(jnp.bfloat16)


def dot3(left, right, contract):
    one = lambda a, b: lax.dot_general(
        a, b, (contract, ((), ())), preferred_element_type=jnp.float32
    )
    return one(left[0], right[0]) + (one(left[0], right[1]) + one(left[1], right[0]))


def pick_kernel(own, asked, pool, *refs):
    packed, done, held, landed, sent = refs[-5:]
    pieces = sent.shape[0]
    part = held.shape[0] // pieces

    def fetch(code, tile, slot):
        row = lax.div(code, own)
        return pltpu.make_async_copy(
            pool.at[lax.div(row, 8), :, lax.rem(row, 8)], held.at[tile, slot], landed
        )

    def start(tile, count):
        for slot in range(8):
            code = asked[tile * (8 // capacity) + slot // capacity, slot % capacity]

            @pl.when(code >= 0)
            def _(code=code, slot=slot):
                fetch(code, tile, slot).start()

            count = count + (code >= 0).astype(jnp.int32)
        return count

    def wait(j, carry):
        fetch(0, 0, 0).wait()
        return carry

    def send(i):
        rows = pl.ds(i * part, part)
        return pltpu.make_async_copy(held.at[rows], packed.at[rows], sent.at[i])

    lax.fori_loop(0, lax.fori_loop(0, held.shape[0], start, 0), wait, 0)
    for i in range(pieces):
        send(i).start()
    done[...] = jnp.zeros_like(done)
    for i in range(pieces):
        send(i).wait()


def pick(asked, own, pool, *earlier):
    total = asked.shape[0] * capacity
    pool_rows, width = pool.shape
    pool = pool.reshape(pool_rows // 8, 8, width // lanes, lanes).transpose(0, 2, 1, 3)
    anywhere = pl.BlockSpec(memory_space=pl.ANY)
    shape = (total // 8, 8, width // lanes, lanes)
    return pl.pallas_call(
        functools.partial(pick_kernel, own),
        in_specs=[pl.BlockSpec(memory_space=pltpu.SMEM), anywhere] + [anywhere] * len(earlier),
        out_specs=[anywhere, pl.BlockSpec(memory_space=pltpu.VMEM)],
        scratch_shapes=[
            pltpu.VMEM(shape, jnp.float32),
            pltpu.SemaphoreType.DMA,
            pltpu.SemaphoreType.DMA((4,)),
        ],
        out_shape=[jax.ShapeDtypeStruct(shape, jnp.float32), jax.ShapeDtypeStruct((8, lanes), jnp.float32)],
        compiler_params=pltpu.CompilerParams(vmem_limit_bytes=limit),
        cost_estimate=pl.CostEstimate(flops=0, bytes_accessed=8 * width * total, transcendentals=0),
    )(asked, pool, *earlier)


def clear_kernel(blank, zeros, fill_sem):
    rows = zeros.shape[0]
    zeros[...] = jnp.zeros_like(zeros)
    fills = [
        pltpu.make_async_copy(zeros, blank.at[pl.ds(i * rows, rows)], fill_sem.at[i])
        for i in range(blank.shape[0] // rows)
    ]
    for fill in fills:
        fill.start()
    for fill in fills:
        fill.wait()


def clear(rows, width, earlier):
    step = 64
    return pl.pallas_call(
        lambda _, *refs: clear_kernel(*refs),
        in_specs=[pl.BlockSpec(memory_space=pl.ANY)],
        out_specs=pl.BlockSpec(memory_space=pl.ANY),
        out_shape=jax.ShapeDtypeStruct((rows, width), jnp.float32),
        scratch_shapes=[pltpu.VMEM((step, width), jnp.float32), pltpu.SemaphoreType.DMA((rows // step,))],
        cost_estimate=pl.CostEstimate(flops=0, bytes_accessed=4 * rows * width, transcendentals=0),
    )(earlier)


def row_fetches(packed, tiles, came, i, step):
    part = pl.ds(i * step, step)
    return [pltpu.make_async_copy(packed.at[:, s, part], tiles.at[:, part, s], came.at[i, s]) for s in range(8)]


def against_kernel(packed, unit, asker, named, *refs):
    parts, scaled, tiles, came = refs[-4:]
    own, count = parts.shape
    strips = tiles.shape[1]
    step = 8
    for i in range(strips // step):
        for fetch in row_fetches(packed, tiles, came, i, step):
            fetch.start()
    real = named[...] >= 0
    scores = jnp.zeros((own, count), jnp.float32)
    squares = jnp.zeros((count, lanes), jnp.float32)
    for i in range(strips // step):
        for fetch in row_fetches(packed, tiles, came, i, step):
            fetch.wait()
        pieces = []
        for j in range(step):
            piece = jnp.where(real, tiles[:, i * step + j].reshape(count, lanes), 0.0)
            squares = squares + piece * piece
            pieces.append(piece)
        columns = slice(i * step * lanes, (i + 1) * step * lanes)
        block = halves(jnp.concatenate(pieces, axis=1))
        scores = scores + dot3(halves(unit[:, columns]), block, ((1,), (1,)))
    scale = lax.rsqrt(jnp.sum(squares, axis=1, keepdims=True) + epsilon)
    scale = jnp.transpose(jnp.broadcast_to(scale, squares.shape))[:own]
    number = lax.broadcasted_iota(jnp.int32, scores.shape, 0)
    chosen = jnp.where(asker[...] == number, jnp.exp(heat * scale * scores - heat), 0.0)
    parts[...] = chosen
    scaled[...] = chosen * scale


def against(packed, unit, asker, *earlier):
    own, width = unit.shape
    groups = packed.shape[0]
    vmem = pl.BlockSpec(memory_space=pltpu.VMEM)
    anywhere = pl.BlockSpec(memory_space=pl.ANY)
    return pl.pallas_call(
        against_kernel,
        in_specs=[anywhere, vmem, vmem, vmem] + [anywhere] * len(earlier),
        out_specs=[vmem, vmem],
        out_shape=[jax.ShapeDtypeStruct((own, 8 * groups), jnp.float32)] * 2,
        scratch_shapes=[
            pltpu.VMEM((groups, width // lanes, 8, lanes), jnp.float32),
            pltpu.SemaphoreType.DMA((width // lanes // 8, 8)),
        ],
        compiler_params=pltpu.CompilerParams(vmem_limit_bytes=limit),
        cost_estimate=pl.CostEstimate(
            flops=48 * own * groups * width, bytes_accessed=32 * width * groups, transcendentals=0
        ),
    )(packed, unit, asker[None, :], jnp.broadcast_to(asker[:, None], (8 * groups, lanes)), *earlier)


def mix_kernel(packed, scaled, named, mixed, tiles, came):
    own, count = scaled.shape
    strips = tiles.shape[1]
    step = 8
    for i in range(strips // step):
        for fetch in row_fetches(packed, tiles, came, i, step):
            fetch.start()
    real = named[...] >= 0
    left = halves(scaled[...])
    for i in range(strips // step):
        for fetch in row_fetches(packed, tiles, came, i, step):
            fetch.wait()
        pieces = [
            jnp.where(real, tiles[:, i * step + j].reshape(count, lanes), 0.0) for j in range(step)
        ]
        columns = slice(i * step * lanes, (i + 1) * step * lanes)
        mixed[:, columns] = dot3(left, halves(jnp.concatenate(pieces, axis=1)), ((1,), (0,)))


def mix(packed, scaled, asker):
    own, count = scaled.shape
    groups, _, strips, _ = packed.shape
    vmem = pl.BlockSpec(memory_space=pltpu.VMEM)
    return pl.pallas_call(
        mix_kernel,
        in_specs=[pl.BlockSpec(memory_space=pl.ANY), vmem, vmem],
        out_specs=vmem,
        out_shape=jax.ShapeDtypeStruct((own, strips * lanes), jnp.float32),
        scratch_shapes=[
            pltpu.VMEM((groups, strips, 8, lanes), jnp.float32),
            pltpu.SemaphoreType.DMA((strips // 8, 8)),
        ],
        compiler_params=pltpu.CompilerParams(vmem_limit_bytes=limit),
        cost_estimate=pl.CostEstimate(
            flops=6 * own * count * strips * lanes, bytes_accessed=4 * count * strips * lanes, transcendentals=0
        ),
    )(packed, scaled, jnp.broadcast_to(asker[:, None], (count, lanes)))


def finish_kernel(
    count, slot_of, row_of, weight, queries, packed, doc_unit, doc_factor, blank,
    doc_grad, pool_grad, held, tiles, upstream, inner, squares, high, low, query_sem, came, row_sem,
):
    slots = inner.shape[0]
    width = queries.shape[1]
    own = doc_unit.shape[0]
    step = 4
    block = step * lanes

    def query_copy(i):
        columns = pl.ds(i * block, block)
        return pltpu.make_async_copy(queries.at[:, columns], held.at[:, columns], query_sem.at[i])

    for i in range(width // block):
        query_copy(i).start()
        for fetch in row_fetches(packed, tiles, came, i, step):
            fetch.start()
    first, second = halves(weight[...])
    high[...] = first
    low[...] = second
    inner[...] = jnp.zeros_like(inner)
    squares[...] = jnp.zeros_like(squares)
    for i in range(width // block):
        columns = slice(i * block, (i + 1) * block)
        query_copy(i).wait()
        above = dot3((high[...], low[...]), halves(held[:, columns]), ((1,), (0,)))
        upstream[:, columns] = above
        for fetch in row_fetches(packed, tiles, came, i, step):
            fetch.wait()
        along, square = inner[...], squares[...]
        for j in range(step):
            piece = tiles[:, i * step + j].reshape(slots, lanes)
            along = along + above[:slots, j * lanes : (j + 1) * lanes] * piece
            square = square + piece * piece
        inner[...] = along
        squares[...] = square

    above = upstream[pl.ds(slots, own), :]
    along = jnp.sum(doc_unit[...] * above, axis=1, keepdims=True)
    doc_grad[...] = doc_factor[:, :1] * (above - doc_unit[...] * along)

    factor = lax.rsqrt(jnp.sum(squares[...], axis=1, keepdims=True) + epsilon)
    along = jnp.sum(inner[...], axis=1, keepdims=True) * factor * factor * factor
    squares[...] = jnp.broadcast_to(factor, squares.shape)
    inner[...] = jnp.broadcast_to(along, inner.shape)

    def row_copy(j):
        return pltpu.make_async_copy(
            upstream.at[pl.ds(slot_of[j], 1)], pool_grad.at[pl.ds(row_of[j], 1)], row_sem
        )

    group = 32

    def settle(tile, sent):
        for i in range(group // 8):
            rows = pl.ds(pl.multiple_of(tile * group + i * 8, 8), 8)
            factor, along = squares[rows, :], inner[rows, :]
            for strip in range(width // lanes):
                columns = slice(strip * lanes, (strip + 1) * lanes)
                upstream[rows, columns] = (
                    factor * upstream[rows, columns] - along * tiles[tile * (group // 8) + i, strip]
                )

        def send(j):
            row_copy(j).start()
            return j + 1

        return lax.while_loop(
            lambda j: (j < count[0]) & (slot_of[jnp.minimum(j, slots - 1)] < (tile + 1) * group), send, sent
        )

    lax.fori_loop(0, slots // group, settle, 0)

    def drain(j, carry):
        row_copy(j).wait()
        return carry

    lax.fori_loop(0, count[0], drain, 0)


def finish(count, slot_of, row_of, weight, queries, packed, doc_unit, doc_factor, blank):
    groups, _, strips, _ = packed.shape
    slots = 8 * groups
    own, width = doc_unit.shape
    batch = queries.shape[0]
    steps = strips // 4
    total = slots + 2 * own
    weight = jnp.pad(weight, ((0, total - weight.shape[0]), (0, 0)))
    vmem = pl.BlockSpec(memory_space=pltpu.VMEM)
    anywhere = pl.BlockSpec(memory_space=pl.ANY)
    smem = pl.BlockSpec(memory_space=pltpu.SMEM)
    return pl.pallas_call(
        finish_kernel,
        in_specs=[smem, smem, smem, vmem, anywhere, anywhere, vmem, vmem, anywhere],
        out_specs=[vmem, anywhere],
        scratch_shapes=[
            pltpu.VMEM((batch, width), jnp.float32),
            pltpu.VMEM((groups, strips, 8, lanes), jnp.float32),
            pltpu.VMEM((total, width), jnp.float32),
            pltpu.VMEM((slots, lanes), jnp.float32),
            pltpu.VMEM((slots, lanes), jnp.float32),
            pltpu.VMEM((total, batch), jnp.bfloat16),
            pltpu.VMEM((total, batch), jnp.bfloat16),
            pltpu.SemaphoreType.DMA((steps,)),
            pltpu.SemaphoreType.DMA((steps, 8)),
            pltpu.SemaphoreType.DMA,
        ],
        out_shape=[
            jax.ShapeDtypeStruct((own, width), jnp.float32),
            jax.ShapeDtypeStruct(blank.shape, jnp.float32),
        ],
        input_output_aliases={8: 1},
        compiler_params=pltpu.CompilerParams(vmem_limit_bytes=limit),
        cost_estimate=pl.CostEstimate(
            flops=6 * total * batch * width, bytes_accessed=4 * width * (batch + 2 * slots), transcendentals=0
        ),
    )(count, slot_of, row_of, weight, queries, packed, doc_unit, doc_factor, blank)


def factor_of(values):
    return lax.rsqrt(jnp.sum(values * values, axis=-1, keepdims=True) + epsilon)


def dot(left, right, contract):
    return lax.dot_general(
        left, right, (contract, ((), ())), precision=highest, preferred_element_type=jnp.float32
    )


def back(factor, unit, upstream):
    return factor * (upstream - unit * jnp.sum(unit * upstream, axis=-1, keepdims=True))


def forward(values, steps):
    return lax.ppermute(values, "pool", [(i, (i + steps) % 4) for i in range(4)])


def ahead(values, direction, size):
    z, x, core = direction
    number = lambda i, j, k: i % 4 * 8 + j % 4 * 2 + k % 2
    blocks = [values]
    for n in range(1, size):
        pairs = [
            (number(i + n * z, j + n * x, k + n * core), number(i, j, k))
            for i in range(4)
            for j in range(4)
            for k in range(2)
        ]
        blocks.append(lax.ppermute(values, "dp", pairs))
    return jnp.concatenate(blocks, axis=0)


def local(queries, documents, document_pool, hard_negatives):
    own, width = queries.shape
    strips = width // lanes
    pool_rows = document_pool.shape[0]
    neg = hard_negatives.shape[1]
    groups = lax.axis_size("dp")
    pool_size = lax.axis_size("pool")
    devices = groups * pool_size
    batch = own * devices
    slots = devices * capacity
    ids = own * neg
    member = lax.axis_index("pool")
    me = lax.axis_index("dp") * pool_size + member

    def exchange(values):
        return lax.all_to_all(values, everyone, split_axis=0, concat_axis=0, tiled=True)

    flat = hard_negatives.reshape(-1)
    owner = flat // pool_rows
    order = jnp.arange(ids, dtype=jnp.int32)
    earlier = (owner[:, None] == owner[None, :]) & (order[None, :] < order[:, None])
    slot = owner * capacity + jnp.sum(earlier.astype(jnp.int32), axis=1)
    asker = order // neg
    taken = slot[None, :] == jnp.arange(slots, dtype=jnp.int32)[:, None]
    code = (flat - owner * pool_rows) * own + asker
    request = jnp.sum(jnp.where(taken, code[None, :] + 1, 0), axis=1) - 1
    slot_query = jnp.sum(jnp.where(taken, asker[None, :] + 1, 0), axis=1) - 1
    request = request.reshape(devices, capacity)
    request = jnp.pad(request, ((0, 0), (0, lanes - capacity)), constant_values=-1)
    asked = exchange(request)

    doc_factor = factor_of(documents)
    doc_unit = documents * doc_factor
    query_factor = factor_of(queries)
    query_unit = queries * query_factor
    everything = lax.all_gather(query_unit, everyone, axis=0, tiled=True)
    passages = ahead(doc_unit, (1, 0, 0), 4)

    cohort = jnp.where(passages[-1, 0] >= -2.0, query_unit, 0.0)
    cohort = jnp.concatenate(
        [cohort] + [forward(cohort, -steps) for steps in range(1, pool_size)], axis=0
    )
    packed, done = pick(asked, own, document_pool, passages, cohort)
    neg_rows = exchange(packed.reshape(devices, capacity * strips, lanes)).reshape(packed.shape)

    picked = done[0, 0] >= 0.0
    arrived = jnp.where(picked, asked[:, :capacity].reshape(-1), -1)
    valid = arrived >= 0
    named_row = jnp.maximum(arrived, 0) // own
    place = jnp.arange(slots, dtype=jnp.int32) // capacity * own + jnp.maximum(arrived, 0) % own
    blank = clear(pool_rows, width, done)

    passages = ahead(ahead(passages, (0, 1, 0), 4), (0, 0, 1), 2)
    parts = jnp.exp(heat * dot(cohort, passages, ((1,), (1,))) - heat)
    sums = jnp.sum(parts, axis=1)

    neg_parts, neg_scaled = against(neg_rows, query_unit, slot_query, sums, blank)

    diagonal = heat * jnp.sum(query_unit * doc_unit, axis=1)
    block = jnp.roll(parts.reshape(pool_size, own, groups * own), member, axis=0)
    block = block.reshape(own * pool_size, groups * own).T.reshape(2, 4, 4, own, own * pool_size)
    block = block.transpose(2, 1, 0, 3, 4)
    for axis, index in enumerate((me // 32, me // 8 % 4, me // 4 % 2)):
        block = jnp.roll(block, index, axis=axis)
    block = block.reshape(groups, 1, -1)
    here = jnp.arange(pool_size, dtype=jnp.int32)[None, :, None] == member
    sums = jnp.roll(sums.reshape(pool_size, own), member, axis=0).reshape(-1)
    news = jnp.concatenate(
        [
            jnp.where(here, block, 0.0).reshape(devices, -1),
            jnp.broadcast_to(sums, (devices, own * pool_size)),
            jnp.broadcast_to(jnp.sum(neg_parts, axis=1), (devices, own)),
            jnp.broadcast_to(diagonal, (devices, own)),
            jnp.sum(neg_parts, axis=0).reshape(devices, capacity),
        ],
        axis=1,
    )
    news = exchange(news)
    edge = own * own * pool_size
    shared = edge + own * pool_size
    both = jnp.sum(news[:, :shared].reshape(groups, pool_size, shared), axis=1)
    doc_parts = both[:, :edge].reshape(groups, own, own * pool_size).transpose(1, 0, 2)
    all_totals = both[:, edge:].reshape(devices, own) + news[:, shared : shared + own]
    all_diagonal = news[:, shared + own : shared + 2 * own]
    slot_parts = news[:, shared + 2 * own :].reshape(-1)
    objective = jnp.sum(jnp.log(all_totals) + heat - all_diagonal) / batch

    scale = heat / all_totals.reshape(1, batch)
    number = jnp.arange(batch, dtype=jnp.int32)[None, :]
    matched = number == me * own + jnp.arange(own, dtype=jnp.int32)[:, None]
    doc_weight = doc_parts.reshape(own, batch) * scale - heat * matched.astype(jnp.float32)
    slot_order = jnp.arange(slots, dtype=jnp.int32)
    spread = jnp.where(place[:, None] == number, slot_parts[:, None], 0.0)
    same = (named_row[:, None] == named_row[None, :]) & valid[None, :]
    spread = dot(same.astype(jnp.float32), spread, ((1,), (0,))) * scale
    repeated = jnp.any(same & (slot_order[None, :] < slot_order[:, None]), axis=1)
    written = valid & ~repeated
    rank = jnp.cumsum(written.astype(jnp.int32)) - 1
    listed = (rank[None, :] == slot_order[:, None]) & written[None, :]
    slot_of = jnp.sum(jnp.where(listed, slot_order[None, :], 0), axis=1)
    row_of = jnp.sum(jnp.where(listed, named_row[None, :], 0), axis=1)
    document_grad, pool_grad = finish(
        jnp.sum(written.astype(jnp.int32))[None],
        slot_of,
        row_of,
        jnp.concatenate([spread, doc_weight], axis=0),
        everything,
        packed,
        doc_unit,
        jnp.broadcast_to(doc_factor, (own, lanes)),
        blank,
    )

    shares = dot(parts, passages, ((1,), (0,)))
    mixed = shares[:own] + mix(neg_rows, neg_scaled, slot_query)
    for steps in range(1, pool_size):
        mixed = mixed + forward(shares[steps * own : (steps + 1) * own], steps)
    total = lax.dynamic_slice(all_totals, (me, 0), (1, own)).reshape(own, 1)
    upstream = heat * (mixed / total - doc_unit)
    query_grad = back(query_factor, query_unit, upstream)
    return (objective, query_grad, document_grad, pool_grad)


def solution(mesh):
    rows = P(everyone, None)
    return jax.shard_map(
        local,
        mesh=mesh,
        in_specs=(rows, rows, rows, rows),
        out_specs=(P(), rows, rows, rows),
        check_vma=False,
    )
```

```python
import functools

import jax
import jax.numpy as jnp
from jax import lax
from jax.experimental import pallas as pl
from jax.experimental.pallas import tpu as pltpu
from jax.sharding import PartitionSpec as P

heat = 20.0
epsilon = 1e-06
highest = lax.Precision.HIGHEST
lanes = 128
everyone = ("dp", "pool")
capacity = 2
limit = 56 * 1024 * 1024


def halves(values):
    high = values.astype(jnp.bfloat16)
    return high, (values - high.astype(jnp.float32)).astype(jnp.bfloat16)


def dot3(left, right, contract):
    one = lambda a, b: lax.dot_general(
        a, b, (contract, ((), ())), preferred_element_type=jnp.float32
    )
    return one(left[0], right[0]) + (one(left[0], right[1]) + one(left[1], right[0]))


def pick_kernel(own, asked, pool, *refs):
    packed, done, held, landed, sent = refs[-5:]
    pieces = sent.shape[0]
    part = held.shape[0] // pieces

    def fetch(code, tile, slot):
        row = lax.div(code, own)
        return pltpu.make_async_copy(
            pool.at[lax.div(row, 8), :, lax.rem(row, 8)], held.at[tile, slot], landed
        )

    def start(tile, count):
        for slot in range(8):
            code = asked[tile * (8 // capacity) + slot // capacity, slot % capacity]

            @pl.when(code >= 0)
            def _(code=code, slot=slot):
                fetch(code, tile, slot).start()

            count = count + (code >= 0).astype(jnp.int32)
        return count

    def wait(j, carry):
        fetch(0, 0, 0).wait()
        return carry

    def send(i):
        rows = pl.ds(i * part, part)
        return pltpu.make_async_copy(held.at[rows], packed.at[rows], sent.at[i])

    lax.fori_loop(0, lax.fori_loop(0, held.shape[0], start, 0), wait, 0)
    for i in range(pieces):
        send(i).start()
    done[...] = jnp.zeros_like(done)
    for i in range(pieces):
        send(i).wait()


def pick(asked, own, pool, *earlier):
    total = asked.shape[0] * capacity
    pool_rows, width = pool.shape
    pool = pool.reshape(pool_rows // 8, 8, width // lanes, lanes).transpose(0, 2, 1, 3)
    anywhere = pl.BlockSpec(memory_space=pl.ANY)
    shape = (total // 8, 8, width // lanes, lanes)
    return pl.pallas_call(
        functools.partial(pick_kernel, own),
        in_specs=[pl.BlockSpec(memory_space=pltpu.SMEM), anywhere] + [anywhere] * len(earlier),
        out_specs=[anywhere, pl.BlockSpec(memory_space=pltpu.VMEM)],
        scratch_shapes=[
            pltpu.VMEM(shape, jnp.float32),
            pltpu.SemaphoreType.DMA,
            pltpu.SemaphoreType.DMA((4,)),
        ],
        out_shape=[jax.ShapeDtypeStruct(shape, jnp.float32), jax.ShapeDtypeStruct((8, lanes), jnp.float32)],
        compiler_params=pltpu.CompilerParams(vmem_limit_bytes=limit),
        cost_estimate=pl.CostEstimate(flops=0, bytes_accessed=8 * width * total, transcendentals=0),
    )(asked, pool, *earlier)


def clear_kernel(blank, zeros, fill_sem):
    rows = zeros.shape[0]
    zeros[...] = jnp.zeros_like(zeros)
    fills = [
        pltpu.make_async_copy(zeros, blank.at[pl.ds(i * rows, rows)], fill_sem.at[i])
        for i in range(blank.shape[0] // rows)
    ]
    for fill in fills:
        fill.start()
    for fill in fills:
        fill.wait()


def clear(rows, width, earlier):
    step = 64
    return pl.pallas_call(
        lambda _, *refs: clear_kernel(*refs),
        in_specs=[pl.BlockSpec(memory_space=pl.ANY)],
        out_specs=pl.BlockSpec(memory_space=pl.ANY),
        out_shape=jax.ShapeDtypeStruct((rows, width), jnp.float32),
        scratch_shapes=[pltpu.VMEM((step, width), jnp.float32), pltpu.SemaphoreType.DMA((rows // step,))],
    )(earlier)


def beside_kernel(queries, documents, parts, shares):
    step = 8 * lanes
    width = queries.shape[1]
    query_squares = jnp.zeros((queries.shape[0], lanes), jnp.float32)
    doc_squares = jnp.zeros((documents.shape[0], lanes), jnp.float32)
    scores = jnp.zeros(parts.shape, jnp.float32)
    for i in range(width // step):
        query, document = (a[:, i * step : (i + 1) * step] for a in (queries, documents))
        for j in range(step // lanes):
            columns = slice(j * lanes, (j + 1) * lanes)
            query_squares = query_squares + query[:, columns] * query[:, columns]
            doc_squares = doc_squares + document[:, columns] * document[:, columns]
        scores = scores + dot3(halves(query), halves(document), ((1,), (1,)))
    query_scale = lax.rsqrt(jnp.sum(query_squares, axis=1, keepdims=True) + epsilon)
    doc_scale = lax.rsqrt(jnp.sum(doc_squares, axis=1, keepdims=True) + epsilon)
    doc_scale = jnp.transpose(jnp.broadcast_to(doc_scale, doc_squares.shape))[: parts.shape[0]]
    chosen = jnp.exp(heat * (scores * (query_scale * doc_scale)) - heat)
    parts[...] = chosen
    left = halves(chosen * doc_scale)
    for i in range(width // step):
        columns = slice(i * step, (i + 1) * step)
        shares[:, columns] = dot3(left, halves(documents[:, columns]), ((1,), (0,)))


def beside(queries, documents):
    vmem = pl.BlockSpec(memory_space=pltpu.VMEM)
    return pl.pallas_call(
        beside_kernel,
        in_specs=[vmem, vmem],
        out_specs=[vmem, vmem],
        out_shape=[
            jax.ShapeDtypeStruct((queries.shape[0], documents.shape[0]), jnp.float32),
            jax.ShapeDtypeStruct(queries.shape, jnp.float32),
        ],
        compiler_params=pltpu.CompilerParams(vmem_limit_bytes=limit),
    )(queries, documents)


def row_fetches(packed, tiles, came, i, step):
    part = pl.ds(i * step, step)
    return [pltpu.make_async_copy(packed.at[:, s, part], tiles.at[:, part, s], came.at[i, s]) for s in range(8)]


def against_kernel(packed, queries, documents, asker, named, *refs):
    parts, scaled, facts, tiles, came = refs[-5:]
    own, count = parts.shape
    strips = tiles.shape[1]
    step = 8
    for i in range(strips // step):
        for fetch in row_fetches(packed, tiles, came, i, step):
            fetch.start()
    query, document = queries[...], documents[...]
    query_scale = lax.rsqrt(jnp.sum(query * query, axis=1, keepdims=True) + epsilon)
    doc_scale = lax.rsqrt(jnp.sum(document * document, axis=1, keepdims=True) + epsilon)
    unit = query * query_scale
    diagonal = heat * jnp.sum(unit * (document * doc_scale), axis=1, keepdims=True)
    lane = lax.broadcasted_iota(jnp.int32, facts.shape, 1)
    facts[...] = jnp.where(lane == 0, query_scale, jnp.where(lane == 1, doc_scale, diagonal))
    real = named[...] >= 0
    scores = jnp.zeros((own, count), jnp.float32)
    squares = jnp.zeros((count, lanes), jnp.float32)
    for i in range(strips // step):
        for fetch in row_fetches(packed, tiles, came, i, step):
            fetch.wait()
        pieces = []
        for j in range(step):
            piece = jnp.where(real, tiles[:, i * step + j].reshape(count, lanes), 0.0)
            squares = squares + piece * piece
            pieces.append(piece)
        columns = slice(i * step * lanes, (i + 1) * step * lanes)
        block = halves(jnp.concatenate(pieces, axis=1))
        scores = scores + dot3(halves(unit[:, columns]), block, ((1,), (1,)))
    scale = lax.rsqrt(jnp.sum(squares, axis=1, keepdims=True) + epsilon)
    scale = jnp.transpose(jnp.broadcast_to(scale, squares.shape))[:own]
    number = lax.broadcasted_iota(jnp.int32, scores.shape, 0)
    chosen = jnp.where(asker[...] == number, jnp.exp(heat * scale * scores - heat), 0.0)
    parts[...] = chosen
    scaled[...] = chosen * scale


def against(packed, queries, documents, asker, *earlier):
    own, width = queries.shape
    groups = packed.shape[0]
    vmem = pl.BlockSpec(memory_space=pltpu.VMEM)
    anywhere = pl.BlockSpec(memory_space=pl.ANY)
    return pl.pallas_call(
        against_kernel,
        in_specs=[anywhere, vmem, vmem, vmem, vmem] + [anywhere] * len(earlier),
        out_specs=[vmem, vmem, vmem],
        out_shape=[jax.ShapeDtypeStruct((own, 8 * groups), jnp.float32)] * 2
        + [jax.ShapeDtypeStruct((own, lanes), jnp.float32)],
        scratch_shapes=[
            pltpu.VMEM((groups, width // lanes, 8, lanes), jnp.float32),
            pltpu.SemaphoreType.DMA((width // lanes // 8, 8)),
        ],
        compiler_params=pltpu.CompilerParams(vmem_limit_bytes=limit),
        cost_estimate=pl.CostEstimate(
            flops=48 * own * groups * width, bytes_accessed=32 * width * groups, transcendentals=0
        ),
    )(packed, queries, documents, asker[None, :], jnp.broadcast_to(asker[:, None], (8 * groups, lanes)), *earlier)


def mix_kernel(packed, scaled, named, mixed, tiles, came):
    own, count = scaled.shape
    strips = tiles.shape[1]
    step = 8
    for i in range(strips // step):
        for fetch in row_fetches(packed, tiles, came, i, step):
            fetch.start()
    real = named[...] >= 0
    left = halves(scaled[...])
    for i in range(strips // step):
        for fetch in row_fetches(packed, tiles, came, i, step):
            fetch.wait()
        pieces = [
            jnp.where(real, tiles[:, i * step + j].reshape(count, lanes), 0.0) for j in range(step)
        ]
        columns = slice(i * step * lanes, (i + 1) * step * lanes)
        mixed[:, columns] = dot3(left, halves(jnp.concatenate(pieces, axis=1)), ((1,), (0,)))


def mix(packed, scaled, asker):
    own, count = scaled.shape
    groups, _, strips, _ = packed.shape
    vmem = pl.BlockSpec(memory_space=pltpu.VMEM)
    return pl.pallas_call(
        mix_kernel,
        in_specs=[pl.BlockSpec(memory_space=pl.ANY), vmem, vmem],
        out_specs=vmem,
        out_shape=jax.ShapeDtypeStruct((own, strips * lanes), jnp.float32),
        scratch_shapes=[
            pltpu.VMEM((groups, strips, 8, lanes), jnp.float32),
            pltpu.SemaphoreType.DMA((strips // 8, 8)),
        ],
        compiler_params=pltpu.CompilerParams(vmem_limit_bytes=limit),
        cost_estimate=pl.CostEstimate(
            flops=6 * own * count * strips * lanes, bytes_accessed=4 * count * strips * lanes, transcendentals=0
        ),
    )(packed, scaled, jnp.broadcast_to(asker[:, None], (count, lanes)))


def finish_kernel(
    count, slot_of, row_of, weight, queries, packed, doc_unit, doc_factor, blank,
    doc_grad, pool_grad, held, tiles, upstream, inner, squares, given, both, query_sem, came, row_sem, given_sem,
):
    slots = inner.shape[0]
    width = queries.shape[1]
    own = doc_unit.shape[0]
    step = 8
    block = step * lanes

    def query_copy(i):
        columns = pl.ds(i * block, block)
        return pltpu.make_async_copy(queries.at[:, columns], held.at[:, columns], query_sem.at[i])

    give = pltpu.make_async_copy(weight, given, given_sem)
    give.start()
    for i in range(width // block):
        query_copy(i).start()
        for fetch in row_fetches(packed, tiles, came, i, step):
            fetch.start()
    give.wait()
    total = given.shape[0]
    first, second = halves(given[...])
    both[:total] = first
    both[total:] = second
    inner[...] = jnp.zeros_like(inner)
    squares[...] = jnp.zeros_like(squares)
    for i in range(width // block):
        columns = slice(i * block, (i + 1) * block)
        query_copy(i).wait()
        high, low = halves(held[:, columns])
        twice = jnp.dot(both[...], high, preferred_element_type=jnp.float32)
        once = jnp.dot(both[:total], low, preferred_element_type=jnp.float32)
        above = twice[:total] + (once + twice[total:])
        upstream[:, columns] = above
        for fetch in row_fetches(packed, tiles, came, i, step):
            fetch.wait()
        along, square = inner[...], squares[...]
        for j in range(step):
            piece = tiles[:, i * step + j].reshape(slots, lanes)
            along = along + above[:slots, j * lanes : (j + 1) * lanes] * piece
            square = square + piece * piece
        inner[...] = along
        squares[...] = square

    above = upstream[pl.ds(slots, own), :]
    along = jnp.sum(doc_unit[...] * above, axis=1, keepdims=True)
    doc_grad[...] = doc_factor[:, :1] * (above - doc_unit[...] * along)

    factor = lax.rsqrt(jnp.sum(squares[...], axis=1, keepdims=True) + epsilon)
    along = jnp.sum(inner[...], axis=1, keepdims=True) * factor * factor * factor
    squares[...] = jnp.broadcast_to(factor, squares.shape)
    inner[...] = jnp.broadcast_to(along, inner.shape)

    def row_copy(j):
        return pltpu.make_async_copy(
            upstream.at[pl.ds(slot_of[j], 1)], pool_grad.at[pl.ds(row_of[j], 1)], row_sem
        )

    group = 32

    def settle(tile, sent):
        for i in range(group // 8):
            rows = pl.ds(pl.multiple_of(tile * group + i * 8, 8), 8)
            factor, along = squares[rows, :], inner[rows, :]
            for strip in range(width // lanes):
                columns = slice(strip * lanes, (strip + 1) * lanes)
                upstream[rows, columns] = (
                    factor * upstream[rows, columns] - along * tiles[tile * (group // 8) + i, strip]
                )

        def send(j):
            row_copy(j).start()
            return j + 1

        return lax.while_loop(
            lambda j: (j < count[0]) & (slot_of[jnp.minimum(j, slots - 1)] < (tile + 1) * group), send, sent
        )

    lax.fori_loop(0, slots // group, settle, 0)

    def drain(j, carry):
        row_copy(j).wait()
        return carry

    lax.fori_loop(0, count[0], drain, 0)


def finish(count, slot_of, row_of, weight, queries, packed, doc_unit, doc_factor, blank):
    groups, _, strips, _ = packed.shape
    slots = 8 * groups
    own, width = doc_unit.shape
    batch = queries.shape[0]
    steps = strips // 8
    total = slots + 2 * own
    weight = jnp.pad(weight, ((0, total - weight.shape[0]), (0, 0)))
    vmem = pl.BlockSpec(memory_space=pltpu.VMEM)
    anywhere = pl.BlockSpec(memory_space=pl.ANY)
    smem = pl.BlockSpec(memory_space=pltpu.SMEM)
    return pl.pallas_call(
        finish_kernel,
        in_specs=[smem, smem, smem, anywhere, anywhere, anywhere, vmem, vmem, anywhere],
        out_specs=[vmem, anywhere],
        scratch_shapes=[
            pltpu.VMEM((batch, width), jnp.float32),
            pltpu.VMEM((groups, strips, 8, lanes), jnp.float32),
            pltpu.VMEM((total, width), jnp.float32),
            pltpu.VMEM((slots, lanes), jnp.float32),
            pltpu.VMEM((slots, lanes), jnp.float32),
            pltpu.VMEM((total, batch), jnp.float32),
            pltpu.VMEM((2 * total, batch), jnp.bfloat16),
            pltpu.SemaphoreType.DMA((steps,)),
            pltpu.SemaphoreType.DMA((steps, 8)),
            pltpu.SemaphoreType.DMA,
            pltpu.SemaphoreType.DMA,
        ],
        out_shape=[
            jax.ShapeDtypeStruct((own, width), jnp.float32),
            jax.ShapeDtypeStruct(blank.shape, jnp.float32),
        ],
        input_output_aliases={8: 1},
        compiler_params=pltpu.CompilerParams(vmem_limit_bytes=limit),
        cost_estimate=pl.CostEstimate(
            flops=6 * total * batch * width, bytes_accessed=4 * width * (batch + 2 * slots), transcendentals=0
        ),
    )(count, slot_of, row_of, weight, queries, packed, doc_unit, doc_factor, blank)


def factor_of(values):
    return lax.rsqrt(jnp.sum(values * values, axis=-1, keepdims=True) + epsilon)


def dot(left, right, contract):
    return lax.dot_general(
        left, right, (contract, ((), ())), precision=highest, preferred_element_type=jnp.float32
    )


def back(factor, unit, upstream):
    return factor * (upstream - unit * jnp.sum(unit * upstream, axis=-1, keepdims=True))


def swap(values, bits):
    return lax.ppermute(values, "pool", [(i, i ^ bits) for i in range(4)])


def by_index(values, member):
    values = values.reshape((2, 2) + values.shape[1:]).swapaxes(0, 1)
    values = jnp.where(member // 2 == 1, values[::-1], values)
    values = jnp.where(member % 2 == 1, values[:, ::-1], values)
    return values.reshape((4,) + values.shape[2:])


def ahead(values, direction, size):
    z, x, core = direction
    number = lambda i, j, k: i % 4 * 8 + j % 4 * 2 + k % 2
    blocks = [values]
    for n in range(1, size):
        pairs = [
            (number(i + n * z, j + n * x, k + n * core), number(i, j, k))
            for i in range(4)
            for j in range(4)
            for k in range(2)
        ]
        blocks.append(lax.ppermute(values, "dp", pairs))
    return jnp.concatenate(blocks, axis=0)


def local(queries, documents, document_pool, hard_negatives):
    own, width = queries.shape
    strips = width // lanes
    pool_rows = document_pool.shape[0]
    neg = hard_negatives.shape[1]
    groups = lax.axis_size("dp")
    pool_size = lax.axis_size("pool")
    devices = groups * pool_size
    batch = own * devices
    slots = devices * capacity
    ids = own * neg
    member = lax.axis_index("pool")
    me = lax.axis_index("dp") * pool_size + member

    def exchange(values):
        return lax.all_to_all(values, everyone, split_axis=0, concat_axis=0, tiled=True)

    flat = hard_negatives.reshape(-1)
    owner = flat // pool_rows
    order = jnp.arange(ids, dtype=jnp.int32)
    earlier = (owner[:, None] == owner[None, :]) & (order[None, :] < order[:, None])
    slot = owner * capacity + jnp.sum(earlier.astype(jnp.int32), axis=1)
    asker = order // neg
    taken = slot[None, :] == jnp.arange(slots, dtype=jnp.int32)[:, None]
    code = (flat - owner * pool_rows) * own + asker
    request = jnp.sum(jnp.where(taken, code[None, :] + 1, 0), axis=1) - 1
    slot_query = jnp.sum(jnp.where(taken, asker[None, :] + 1, 0), axis=1) - 1
    request = request.reshape(devices, capacity)
    request = jnp.pad(request, ((0, 0), (0, lanes - capacity)), constant_values=-1)
    asked = exchange(request)

    everything = lax.all_gather(queries, everyone, axis=0, tiled=True)
    passages = ahead(documents, (1, 0, 0), 4)
    cohort = jnp.concatenate([queries, swap(queries, 2)], axis=0)
    cohort = jnp.concatenate([cohort, swap(cohort, 1)], axis=0)
    packed, done = pick(asked, own, document_pool, passages, cohort)
    neg_rows = exchange(packed.reshape(devices, capacity * strips, lanes)).reshape(packed.shape)

    picked = done[0, 0] >= 0.0
    arrived = jnp.where(picked, asked[:, :capacity].reshape(-1), -1)
    valid = arrived >= 0
    named_row = jnp.maximum(arrived, 0) // own
    place = jnp.arange(slots, dtype=jnp.int32) // capacity * own + jnp.maximum(arrived, 0) % own
    blank = clear(pool_rows, width, done)

    passages = ahead(ahead(passages, (0, 1, 0), 4), (0, 0, 1), 2)
    parts, shares = beside(cohort, passages)
    sums = jnp.sum(parts, axis=1)

    neg_parts, neg_scaled, facts = against(neg_rows, queries, documents, slot_query, sums, blank)
    query_factor, doc_factor, diagonal = facts[:, 0:1], facts[:, 1:2], facts[:, 2]
    query_unit = queries * query_factor
    doc_unit = documents * doc_factor

    block = by_index(parts.reshape(pool_size, own, groups * own), member)
    block = block.reshape(own * pool_size, groups * own).T.reshape(2, 4, 4, own, own * pool_size)
    block = block.transpose(2, 1, 0, 3, 4)
    for axis, index in enumerate((me // 32, me // 8 % 4, me // 4 % 2)):
        block = jnp.roll(block, index, axis=axis)
    block = block.reshape(groups, 1, -1)
    here = jnp.arange(pool_size, dtype=jnp.int32)[None, :, None] == member
    sums = by_index(sums.reshape(pool_size, own), member).reshape(-1)
    news = jnp.concatenate(
        [
            jnp.where(here, block, 0.0).reshape(devices, -1),
            jnp.broadcast_to(sums, (devices, own * pool_size)),
            jnp.broadcast_to(jnp.sum(neg_parts, axis=1), (devices, own)),
            jnp.broadcast_to(diagonal, (devices, own)),
            jnp.broadcast_to(query_factor.reshape(1, own), (devices, own)),
            jnp.sum(neg_parts, axis=0).reshape(devices, capacity),
        ],
        axis=1,
    )
    news = exchange(news)
    edge = own * own * pool_size
    shared = edge + own * pool_size
    both = jnp.sum(news[:, :shared].reshape(groups, pool_size, shared), axis=1)
    doc_parts = both[:, :edge].reshape(groups, own, own * pool_size).transpose(1, 0, 2)
    all_totals = both[:, edge:].reshape(devices, own) + news[:, shared : shared + own]
    all_diagonal = news[:, shared + own : shared + 2 * own]
    all_factors = news[:, shared + 2 * own : shared + 3 * own].reshape(1, batch)
    slot_parts = news[:, shared + 3 * own :].reshape(-1)
    objective = jnp.sum(jnp.log(all_totals) + heat - all_diagonal) / batch

    scale = heat * all_factors / all_totals.reshape(1, batch)
    number = jnp.arange(batch, dtype=jnp.int32)[None, :]
    matched = number == me * own + jnp.arange(own, dtype=jnp.int32)[:, None]
    doc_weight = doc_parts.reshape(own, batch) * scale - jnp.where(matched, heat * all_factors, 0.0)
    slot_order = jnp.arange(slots, dtype=jnp.int32)
    spread = jnp.where(place[:, None] == number, slot_parts[:, None], 0.0)
    same = (named_row[:, None] == named_row[None, :]) & valid[None, :]
    spread = dot(same.astype(jnp.float32), spread, ((1,), (0,))) * scale
    repeated = jnp.any(same & (slot_order[None, :] < slot_order[:, None]), axis=1)
    written = valid & ~repeated
    rank = jnp.cumsum(written.astype(jnp.int32)) - 1
    listed = (rank[None, :] == slot_order[:, None]) & written[None, :]
    slot_of = jnp.sum(jnp.where(listed, slot_order[None, :], 0), axis=1)
    row_of = jnp.sum(jnp.where(listed, named_row[None, :], 0), axis=1)
    document_grad, pool_grad = finish(
        jnp.sum(written.astype(jnp.int32))[None],
        slot_of,
        row_of,
        jnp.concatenate([spread, doc_weight], axis=0),
        everything,
        packed,
        doc_unit,
        jnp.broadcast_to(doc_factor, (own, lanes)),
        blank,
    )

    mixed = shares[:own] + mix(neg_rows, neg_scaled, slot_query)
    for i, bits in ((1, 2), (2, 1), (3, 3)):
        mixed = mixed + swap(shares[i * own : (i + 1) * own], bits)
    total = lax.dynamic_slice(all_totals, (me, 0), (1, own)).reshape(own, 1)
    upstream = heat * (mixed / total - doc_unit)
    query_grad = back(query_factor, query_unit, upstream)
    return (objective, query_grad, document_grad, pool_grad)


def solution(mesh):
    rows = P(everyone, None)
    return jax.shard_map(
        local,
        mesh=mesh,
        in_specs=(rows, rows, rows, rows),
        out_specs=(P(), rows, rows, rows),
        check_vma=False,
    )
```

```python
import functools

import jax
import jax.numpy as jnp
from jax import lax
from jax.experimental import pallas as pl
from jax.experimental.pallas import tpu as pltpu
from jax.sharding import PartitionSpec as P

heat = 20.0
epsilon = 1e-06
highest = lax.Precision.HIGHEST
lanes = 128
everyone = ("dp", "pool")
capacity = 2
limit = 56 * 1024 * 1024


def halves(values):
    high = values.astype(jnp.bfloat16)
    return high, (values - high.astype(jnp.float32)).astype(jnp.bfloat16)


def dot3(left, right, contract):
    one = lambda a, b: lax.dot_general(
        a, b, (contract, ((), ())), preferred_element_type=jnp.float32
    )
    return one(left[0], right[0]) + (one(left[0], right[1]) + one(left[1], right[0]))


def pick_kernel(own, asked, pool, *refs):
    packed, done, held, landed, sent = refs[-5:]
    pieces = sent.shape[0]
    part = held.shape[0] // pieces

    def fetch(code, tile, slot):
        row = lax.div(code, own)
        return pltpu.make_async_copy(
            pool.at[lax.div(row, 8), :, lax.rem(row, 8)], held.at[tile, slot], landed.at[lax.div(tile, part)]
        )

    def start(tile, count):
        for slot in range(8):
            code = asked[tile * (8 // capacity) + slot // capacity, slot % capacity]

            @pl.when(code >= 0)
            def _(code=code, slot=slot):
                fetch(code, tile, slot).start()

            count = count + (code >= 0).astype(jnp.int32)
        return count

    def send(i):
        rows = pl.ds(i * part, part)
        return pltpu.make_async_copy(held.at[rows], packed.at[rows], sent.at[i])

    counts = [lax.fori_loop(i * part, (i + 1) * part, start, 0) for i in range(pieces)]
    for i in range(pieces):

        def wait(j, carry, i=i):
            fetch(0, i * part, 0).wait()
            return carry

        lax.fori_loop(0, counts[i], wait, 0)
        send(i).start()
    done[...] = jnp.zeros_like(done)
    for i in range(pieces):
        send(i).wait()


def pick(asked, own, pool, *earlier):
    total = asked.shape[0] * capacity
    pool_rows, width = pool.shape
    pool = pool.reshape(pool_rows // 8, 8, width // lanes, lanes).transpose(0, 2, 1, 3)
    anywhere = pl.BlockSpec(memory_space=pl.ANY)
    shape = (total // 8, 8, width // lanes, lanes)
    return pl.pallas_call(
        functools.partial(pick_kernel, own),
        in_specs=[pl.BlockSpec(memory_space=pltpu.SMEM), anywhere] + [anywhere] * len(earlier),
        out_specs=[anywhere, pl.BlockSpec(memory_space=pltpu.VMEM)],
        scratch_shapes=[
            pltpu.VMEM(shape, jnp.float32),
            pltpu.SemaphoreType.DMA((4,)),
            pltpu.SemaphoreType.DMA((4,)),
        ],
        out_shape=[jax.ShapeDtypeStruct(shape, jnp.float32), jax.ShapeDtypeStruct((8, lanes), jnp.float32)],
        compiler_params=pltpu.CompilerParams(vmem_limit_bytes=limit),
        cost_estimate=pl.CostEstimate(flops=0, bytes_accessed=8 * width * total, transcendentals=0),
    )(asked, pool, *earlier)


def clear_kernel(blank, zeros, fill_sem):
    rows = zeros.shape[0]
    zeros[...] = jnp.zeros_like(zeros)
    fills = [
        pltpu.make_async_copy(zeros, blank.at[pl.ds(i * rows, rows)], fill_sem.at[i])
        for i in range(blank.shape[0] // rows)
    ]
    for fill in fills:
        fill.start()
    for fill in fills:
        fill.wait()


def clear(rows, width, earlier):
    step = 64
    return pl.pallas_call(
        lambda _, *refs: clear_kernel(*refs),
        in_specs=[pl.BlockSpec(memory_space=pl.ANY)],
        out_specs=pl.BlockSpec(memory_space=pl.ANY),
        out_shape=jax.ShapeDtypeStruct((rows, width), jnp.float32),
        scratch_shapes=[pltpu.VMEM((step, width), jnp.float32), pltpu.SemaphoreType.DMA((rows // step,))],
    )(earlier)


def beside_kernel(queries, documents, parts, shares):
    step = 8 * lanes
    width = queries.shape[1]
    query_squares = jnp.zeros((queries.shape[0], lanes), jnp.float32)
    doc_squares = jnp.zeros((documents.shape[0], lanes), jnp.float32)
    scores = jnp.zeros(parts.shape, jnp.float32)
    for i in range(width // step):
        query, document = (a[:, i * step : (i + 1) * step] for a in (queries, documents))
        for j in range(step // lanes):
            columns = slice(j * lanes, (j + 1) * lanes)
            query_squares = query_squares + query[:, columns] * query[:, columns]
            doc_squares = doc_squares + document[:, columns] * document[:, columns]
        scores = scores + dot3(halves(query), halves(document), ((1,), (1,)))
    query_scale = lax.rsqrt(jnp.sum(query_squares, axis=1, keepdims=True) + epsilon)
    doc_scale = lax.rsqrt(jnp.sum(doc_squares, axis=1, keepdims=True) + epsilon)
    doc_scale = jnp.transpose(jnp.broadcast_to(doc_scale, doc_squares.shape))[: parts.shape[0]]
    chosen = jnp.exp(heat * (scores * (query_scale * doc_scale)) - heat)
    parts[...] = chosen
    left = halves(chosen * doc_scale)
    for i in range(width // step):
        columns = slice(i * step, (i + 1) * step)
        shares[:, columns] = dot3(left, halves(documents[:, columns]), ((1,), (0,)))


def beside(queries, documents):
    vmem = pl.BlockSpec(memory_space=pltpu.VMEM)
    return pl.pallas_call(
        beside_kernel,
        in_specs=[vmem, vmem],
        out_specs=[vmem, vmem],
        out_shape=[
            jax.ShapeDtypeStruct((queries.shape[0], documents.shape[0]), jnp.float32),
            jax.ShapeDtypeStruct(queries.shape, jnp.float32),
        ],
        compiler_params=pltpu.CompilerParams(vmem_limit_bytes=limit),
    )(queries, documents)


def row_fetches(packed, tiles, came, i, step):
    part = pl.ds(i * step, step)
    return [pltpu.make_async_copy(packed.at[:, s, part], tiles.at[:, part, s], came.at[i, s]) for s in range(8)]


def against_kernel(packed, queries, documents, asker, named, *refs):
    parts, scaled, facts, tiles, came = refs[-5:]
    own, count = parts.shape
    strips = tiles.shape[1]
    step = 8
    for i in range(strips // step):
        for fetch in row_fetches(packed, tiles, came, i, step):
            fetch.start()
    query, document = queries[...], documents[...]
    query_scale = lax.rsqrt(jnp.sum(query * query, axis=1, keepdims=True) + epsilon)
    doc_scale = lax.rsqrt(jnp.sum(document * document, axis=1, keepdims=True) + epsilon)
    unit = query * query_scale
    diagonal = heat * jnp.sum(unit * (document * doc_scale), axis=1, keepdims=True)
    lane = lax.broadcasted_iota(jnp.int32, facts.shape, 1)
    facts[...] = jnp.where(lane == 0, query_scale, jnp.where(lane == 1, doc_scale, diagonal))
    real = named[...] >= 0
    scores = jnp.zeros((own, count), jnp.float32)
    squares = jnp.zeros((count, lanes), jnp.float32)
    for i in range(strips // step):
        for fetch in row_fetches(packed, tiles, came, i, step):
            fetch.wait()
        pieces = []
        for j in range(step):
            piece = jnp.where(real, tiles[:, i * step + j].reshape(count, lanes), 0.0)
            squares = squares + piece * piece
            pieces.append(piece)
        columns = slice(i * step * lanes, (i + 1) * step * lanes)
        block = halves(jnp.concatenate(pieces, axis=1))
        scores = scores + dot3(halves(unit[:, columns]), block, ((1,), (1,)))
    scale = lax.rsqrt(jnp.sum(squares, axis=1, keepdims=True) + epsilon)
    scale = jnp.transpose(jnp.broadcast_to(scale, squares.shape))[:own]
    number = lax.broadcasted_iota(jnp.int32, scores.shape, 0)
    chosen = jnp.where(asker[...] == number, jnp.exp(heat * scale * scores - heat), 0.0)
    parts[...] = chosen
    scaled[...] = chosen * scale


def against(packed, queries, documents, asker, *earlier):
    own, width = queries.shape
    groups = packed.shape[0]
    vmem = pl.BlockSpec(memory_space=pltpu.VMEM)
    anywhere = pl.BlockSpec(memory_space=pl.ANY)
    return pl.pallas_call(
        against_kernel,
        in_specs=[anywhere, vmem, vmem, vmem, vmem] + [anywhere] * len(earlier),
        out_specs=[vmem, vmem, vmem],
        out_shape=[jax.ShapeDtypeStruct((own, 8 * groups), jnp.float32)] * 2
        + [jax.ShapeDtypeStruct((own, lanes), jnp.float32)],
        scratch_shapes=[
            pltpu.VMEM((groups, width // lanes, 8, lanes), jnp.float32),
            pltpu.SemaphoreType.DMA((width // lanes // 8, 8)),
        ],
        compiler_params=pltpu.CompilerParams(vmem_limit_bytes=limit),
        cost_estimate=pl.CostEstimate(
            flops=48 * own * groups * width, bytes_accessed=32 * width * groups, transcendentals=0
        ),
    )(packed, queries, documents, asker[None, :], jnp.broadcast_to(asker[:, None], (8 * groups, lanes)), *earlier)


def mix_kernel(packed, scaled, named, mixed, tiles, came):
    own, count = scaled.shape
    strips = tiles.shape[1]
    step = 8
    for i in range(strips // step):
        for fetch in row_fetches(packed, tiles, came, i, step):
            fetch.start()
    real = named[...] >= 0
    left = halves(scaled[...])
    for i in range(strips // step):
        for fetch in row_fetches(packed, tiles, came, i, step):
            fetch.wait()
        pieces = [
            jnp.where(real, tiles[:, i * step + j].reshape(count, lanes), 0.0) for j in range(step)
        ]
        columns = slice(i * step * lanes, (i + 1) * step * lanes)
        mixed[:, columns] = dot3(left, halves(jnp.concatenate(pieces, axis=1)), ((1,), (0,)))


def mix(packed, scaled, asker):
    own, count = scaled.shape
    groups, _, strips, _ = packed.shape
    vmem = pl.BlockSpec(memory_space=pltpu.VMEM)
    return pl.pallas_call(
        mix_kernel,
        in_specs=[pl.BlockSpec(memory_space=pl.ANY), vmem, vmem],
        out_specs=vmem,
        out_shape=jax.ShapeDtypeStruct((own, strips * lanes), jnp.float32),
        scratch_shapes=[
            pltpu.VMEM((groups, strips, 8, lanes), jnp.float32),
            pltpu.SemaphoreType.DMA((strips // 8, 8)),
        ],
        compiler_params=pltpu.CompilerParams(vmem_limit_bytes=limit),
        cost_estimate=pl.CostEstimate(
            flops=6 * own * count * strips * lanes, bytes_accessed=4 * count * strips * lanes, transcendentals=0
        ),
    )(packed, scaled, jnp.broadcast_to(asker[:, None], (count, lanes)))


def finish_kernel(
    count, slot_of, row_of, weight, queries, packed, doc_unit, doc_factor, blank,
    doc_grad, pool_grad, held, tiles, upstream, inner, squares, given, both, query_sem, came, row_sem, given_sem,
):
    slots = inner.shape[0]
    width = queries.shape[1]
    own = doc_unit.shape[0]
    step = 8
    block = step * lanes

    def query_copy(i):
        columns = pl.ds(i * block, block)
        return pltpu.make_async_copy(queries.at[:, columns], held.at[:, columns], query_sem.at[i])

    give = pltpu.make_async_copy(weight, given, given_sem)
    give.start()
    for i in range(width // block):
        query_copy(i).start()
        for fetch in row_fetches(packed, tiles, came, i, step):
            fetch.start()
    give.wait()
    total = given.shape[0]
    first, second = halves(given[...])
    both[:total] = first
    both[total:] = second
    inner[...] = jnp.zeros_like(inner)
    squares[...] = jnp.zeros_like(squares)
    for i in range(width // block):
        columns = slice(i * block, (i + 1) * block)
        query_copy(i).wait()
        high, low = halves(held[:, columns])
        twice = jnp.dot(both[...], high, preferred_element_type=jnp.float32)
        once = jnp.dot(both[:total], low, preferred_element_type=jnp.float32)
        above = twice[:total] + (once + twice[total:])
        upstream[:, columns] = above
        for fetch in row_fetches(packed, tiles, came, i, step):
            fetch.wait()
        along, square = inner[...], squares[...]
        for j in range(step):
            piece = tiles[:, i * step + j].reshape(slots, lanes)
            along = along + above[:slots, j * lanes : (j + 1) * lanes] * piece
            square = square + piece * piece
        inner[...] = along
        squares[...] = square

    above = upstream[pl.ds(slots, own), :]
    along = jnp.sum(doc_unit[...] * above, axis=1, keepdims=True)
    doc_grad[...] = doc_factor[:, :1] * (above - doc_unit[...] * along)

    factor = lax.rsqrt(jnp.sum(squares[...], axis=1, keepdims=True) + epsilon)
    along = jnp.sum(inner[...], axis=1, keepdims=True) * factor * factor * factor
    squares[...] = jnp.broadcast_to(factor, squares.shape)
    inner[...] = jnp.broadcast_to(along, inner.shape)

    def row_copy(j):
        return pltpu.make_async_copy(
            upstream.at[pl.ds(slot_of[j], 1)], pool_grad.at[pl.ds(row_of[j], 1)], row_sem
        )

    group = 32

    def settle(tile, sent):
        for i in range(group // 8):
            rows = pl.ds(pl.multiple_of(tile * group + i * 8, 8), 8)
            factor, along = squares[rows, :], inner[rows, :]
            for strip in range(width // lanes):
                columns = slice(strip * lanes, (strip + 1) * lanes)
                upstream[rows, columns] = (
                    factor * upstream[rows, columns] - along * tiles[tile * (group // 8) + i, strip]
                )

        def send(j):
            row_copy(j).start()
            return j + 1

        return lax.while_loop(
            lambda j: (j < count[0]) & (slot_of[jnp.minimum(j, slots - 1)] < (tile + 1) * group), send, sent
        )

    lax.fori_loop(0, slots // group, settle, 0)

    def drain(j, carry):
        row_copy(j).wait()
        return carry

    lax.fori_loop(0, count[0], drain, 0)


def finish(count, slot_of, row_of, weight, queries, packed, doc_unit, doc_factor, blank):
    groups, _, strips, _ = packed.shape
    slots = 8 * groups
    own, width = doc_unit.shape
    batch = queries.shape[0]
    steps = strips // 8
    total = slots + 2 * own
    weight = jnp.pad(weight, ((0, total - weight.shape[0]), (0, 0)))
    vmem = pl.BlockSpec(memory_space=pltpu.VMEM)
    anywhere = pl.BlockSpec(memory_space=pl.ANY)
    smem = pl.BlockSpec(memory_space=pltpu.SMEM)
    return pl.pallas_call(
        finish_kernel,
        in_specs=[smem, smem, smem, anywhere, anywhere, anywhere, vmem, vmem, anywhere],
        out_specs=[vmem, anywhere],
        scratch_shapes=[
            pltpu.VMEM((batch, width), jnp.float32),
            pltpu.VMEM((groups, strips, 8, lanes), jnp.float32),
            pltpu.VMEM((total, width), jnp.float32),
            pltpu.VMEM((slots, lanes), jnp.float32),
            pltpu.VMEM((slots, lanes), jnp.float32),
            pltpu.VMEM((total, batch), jnp.float32),
            pltpu.VMEM((2 * total, batch), jnp.bfloat16),
            pltpu.SemaphoreType.DMA((steps,)),
            pltpu.SemaphoreType.DMA((steps, 8)),
            pltpu.SemaphoreType.DMA,
            pltpu.SemaphoreType.DMA,
        ],
        out_shape=[
            jax.ShapeDtypeStruct((own, width), jnp.float32),
            jax.ShapeDtypeStruct(blank.shape, jnp.float32),
        ],
        input_output_aliases={8: 1},
        compiler_params=pltpu.CompilerParams(vmem_limit_bytes=limit),
        cost_estimate=pl.CostEstimate(
            flops=6 * total * batch * width, bytes_accessed=4 * width * (batch + 2 * slots), transcendentals=0
        ),
    )(count, slot_of, row_of, weight, queries, packed, doc_unit, doc_factor, blank)


def factor_of(values):
    return lax.rsqrt(jnp.sum(values * values, axis=-1, keepdims=True) + epsilon)


def dot(left, right, contract):
    return lax.dot_general(
        left, right, (contract, ((), ())), precision=highest, preferred_element_type=jnp.float32
    )


def back(factor, unit, upstream):
    return factor * (upstream - unit * jnp.sum(unit * upstream, axis=-1, keepdims=True))


def swap(values, bits):
    return lax.ppermute(values, "pool", [(i, i ^ bits) for i in range(4)])


def by_index(values, member):
    values = values.reshape((2, 2) + values.shape[1:]).swapaxes(0, 1)
    values = jnp.where(member // 2 == 1, values[::-1], values)
    values = jnp.where(member % 2 == 1, values[:, ::-1], values)
    return values.reshape((4,) + values.shape[2:])


def ahead(values, direction, size):
    z, x, core = direction
    number = lambda i, j, k: i % 4 * 8 + j % 4 * 2 + k % 2
    blocks = [values]
    for n in range(1, size):
        pairs = [
            (number(i + n * z, j + n * x, k + n * core), number(i, j, k))
            for i in range(4)
            for j in range(4)
            for k in range(2)
        ]
        blocks.append(lax.ppermute(values, "dp", pairs))
    return jnp.concatenate(blocks, axis=0)


def local(queries, documents, document_pool, hard_negatives):
    own, width = queries.shape
    strips = width // lanes
    pool_rows = document_pool.shape[0]
    neg = hard_negatives.shape[1]
    groups = lax.axis_size("dp")
    pool_size = lax.axis_size("pool")
    devices = groups * pool_size
    batch = own * devices
    slots = devices * capacity
    ids = own * neg
    member = lax.axis_index("pool")
    me = lax.axis_index("dp") * pool_size + member

    def exchange(values):
        return lax.all_to_all(values, everyone, split_axis=0, concat_axis=0, tiled=True)

    flat = hard_negatives.reshape(-1)
    owner = flat // pool_rows
    order = jnp.arange(ids, dtype=jnp.int32)
    earlier = (owner[:, None] == owner[None, :]) & (order[None, :] < order[:, None])
    slot = owner * capacity + jnp.sum(earlier.astype(jnp.int32), axis=1)
    asker = order // neg
    taken = slot[None, :] == jnp.arange(slots, dtype=jnp.int32)[:, None]
    code = (flat - owner * pool_rows) * own + asker
    request = jnp.sum(jnp.where(taken, code[None, :] + 1, 0), axis=1) - 1
    slot_query = jnp.sum(jnp.where(taken, asker[None, :] + 1, 0), axis=1) - 1
    request = request.reshape(devices, capacity)
    request = jnp.pad(request, ((0, 0), (0, lanes - capacity)), constant_values=-1)
    asked = exchange(request)

    everything = lax.all_gather(queries, everyone, axis=0, tiled=True)
    passages = ahead(documents, (1, 0, 0), 4)
    cohort = jnp.concatenate([queries, swap(queries, 2)], axis=0)
    cohort = jnp.concatenate([cohort, swap(cohort, 1)], axis=0)
    packed, done = pick(asked, own, document_pool, passages, cohort)
    neg_rows = exchange(packed.reshape(devices, capacity * strips, lanes)).reshape(packed.shape)

    picked = done[0, 0] >= 0.0
    arrived = jnp.where(picked, asked[:, :capacity].reshape(-1), -1)
    valid = arrived >= 0
    named_row = jnp.maximum(arrived, 0) // own
    place = jnp.arange(slots, dtype=jnp.int32) // capacity * own + jnp.maximum(arrived, 0) % own
    blank = clear(pool_rows, width, done)

    passages = ahead(ahead(passages, (0, 1, 0), 4), (0, 0, 1), 2)
    parts, shares = beside(cohort, passages)
    sums = jnp.sum(parts, axis=1)

    neg_parts, neg_scaled, facts = against(neg_rows, queries, documents, slot_query, sums, blank)
    query_factor, doc_factor, diagonal = facts[:, 0:1], facts[:, 1:2], facts[:, 2]
    query_unit = queries * query_factor
    doc_unit = documents * doc_factor

    block = by_index(parts.reshape(pool_size, own, groups * own), member)
    block = block.reshape(own * pool_size, groups * own).T.reshape(2, 4, 4, own, own * pool_size)
    block = block.transpose(2, 1, 0, 3, 4)
    for axis, index in enumerate((me // 32, me // 8 % 4, me // 4 % 2)):
        block = jnp.roll(block, index, axis=axis)
    block = block.reshape(groups, 1, -1)
    here = jnp.arange(pool_size, dtype=jnp.int32)[None, :, None] == member
    sums = by_index(sums.reshape(pool_size, own), member).reshape(-1)
    news = jnp.concatenate(
        [
            jnp.where(here, block, 0.0).reshape(devices, -1),
            jnp.broadcast_to(sums, (devices, own * pool_size)),
            jnp.broadcast_to(jnp.sum(neg_parts, axis=1), (devices, own)),
            jnp.broadcast_to(diagonal, (devices, own)),
            jnp.broadcast_to(query_factor.reshape(1, own), (devices, own)),
            jnp.sum(neg_parts, axis=0).reshape(devices, capacity),
        ],
        axis=1,
    )
    news = exchange(news)
    edge = own * own * pool_size
    shared = edge + own * pool_size
    both = jnp.sum(news[:, :shared].reshape(groups, pool_size, shared), axis=1)
    doc_parts = both[:, :edge].reshape(groups, own, own * pool_size).transpose(1, 0, 2)
    all_totals = both[:, edge:].reshape(devices, own) + news[:, shared : shared + own]
    all_diagonal = news[:, shared + own : shared + 2 * own]
    all_factors = news[:, shared + 2 * own : shared + 3 * own].reshape(1, batch)
    slot_parts = news[:, shared + 3 * own :].reshape(-1)
    objective = jnp.sum(jnp.log(all_totals) + heat - all_diagonal) / batch

    scale = heat * all_factors / all_totals.reshape(1, batch)
    number = jnp.arange(batch, dtype=jnp.int32)[None, :]
    matched = number == me * own + jnp.arange(own, dtype=jnp.int32)[:, None]
    doc_weight = doc_parts.reshape(own, batch) * scale - jnp.where(matched, heat * all_factors, 0.0)
    slot_order = jnp.arange(slots, dtype=jnp.int32)
    spread = jnp.where(place[:, None] == number, slot_parts[:, None], 0.0)
    same = (named_row[:, None] == named_row[None, :]) & valid[None, :]
    spread = dot(same.astype(jnp.float32), spread, ((1,), (0,))) * scale
    repeated = jnp.any(same & (slot_order[None, :] < slot_order[:, None]), axis=1)
    written = valid & ~repeated
    rank = jnp.cumsum(written.astype(jnp.int32)) - 1
    listed = (rank[None, :] == slot_order[:, None]) & written[None, :]
    slot_of = jnp.sum(jnp.where(listed, slot_order[None, :], 0), axis=1)
    row_of = jnp.sum(jnp.where(listed, named_row[None, :], 0), axis=1)
    document_grad, pool_grad = finish(
        jnp.sum(written.astype(jnp.int32))[None],
        slot_of,
        row_of,
        jnp.concatenate([spread, doc_weight], axis=0),
        everything,
        packed,
        doc_unit,
        jnp.broadcast_to(doc_factor, (own, lanes)),
        blank,
    )

    mixed = shares[:own] + mix(neg_rows, neg_scaled, slot_query)
    for i, bits in ((1, 2), (2, 1), (3, 3)):
        mixed = mixed + swap(shares[i * own : (i + 1) * own], bits)
    total = lax.dynamic_slice(all_totals, (me, 0), (1, own)).reshape(own, 1)
    upstream = heat * (mixed / total - doc_unit)
    query_grad = back(query_factor, query_unit, upstream)
    return (objective, query_grad, document_grad, pool_grad)


def solution(mesh):
    rows = P(everyone, None)
    return jax.shard_map(
        local,
        mesh=mesh,
        in_specs=(rows, rows, rows, rows),
        out_specs=(P(), rows, rows, rows),
        check_vma=False,
    )
```
